128 devices in a mesh: seq: 16 (over z, y), fsdp: 8 (over x, core).
Axes of the slice: x: 4, y: 4, z: 4, core: 2. Of those that a mesh axis runs over, the one named last changes fastest.
Arguments:
- inputs: float32 [8, 2048, 1024], P('fsdp', 'seq'), may hold values from -6 to 6
- cotangent: float32 [8, 2048, 1024], P('fsdp', 'seq'), may hold values from -6 to 6
- lengths: int32 [8, 4], P('fsdp'), may hold values from 1 to 1921, 2048 in all within a row
- seq_order: int32 [8, 4], P('fsdp'), may hold values from 0 to 3, each once within a row
- first_gain: float32 [1024], P(('seq', 'fsdp')), may hold values from 0.25 to 1.75
- first_shift: float32 [1024], P(('seq', 'fsdp')), may hold values from -4 to 4
- joined_weight: float32 [1024, 3072], P(('seq', 'fsdp')), may hold values from -0.1875 to 0.1875
- joined_bias: float32 [2048], P(('seq', 'fsdp')), may hold values from -4 to 4
- dense_weight: float32 [1024, 1024], P(('seq', 'fsdp')), may hold values from -0.5 to 0.5
- dense_bias: float32 [1024], P(('seq', 'fsdp')), may hold values from -4 to 4
- second_gain: float32 [1024], P(('seq', 'fsdp')), may hold values from 0.25 to 1.75
- second_shift: float32 [1024], P(('seq', 'fsdp')), may hold values from -4 to 4
- up_weight: float32 [1024, 4096], P(('seq', 'fsdp')), may hold values from -0.1875 to 0.1875
- up_bias: float32 [4096], P(('seq', 'fsdp')), may hold values from -4 to 4
- down_weight: float32 [4096, 1024], P(('seq', 'fsdp')), may hold values from -0.09375 to 0.09375
- down_bias: float32 [1024], P(('seq', 'fsdp')), may hold values from -4 to 4
Outputs:
- output: float32 [8, 2048, 1024], P('fsdp', 'seq')
- input_grad: float32 [8, 2048, 1024], P('fsdp', 'seq')
- first_gain_grad: float32 [1024], P(('seq', 'fsdp'))
- first_shift_grad: float32 [1024], P(('seq', 'fsdp'))
- joined_weight_grad: float32 [1024, 3072], P(('seq', 'fsdp'))
- joined_bias_grad: float32 [2048], P(('seq', 'fsdp'))
- dense_weight_grad: float32 [1024, 1024], P(('seq', 'fsdp'))
- dense_bias_grad: float32 [1024], P(('seq', 'fsdp'))
- second_gain_grad: float32 [1024], P(('seq', 'fsdp'))
- second_shift_grad: float32 [1024], P(('seq', 'fsdp'))
- up_weight_grad: float32 [1024, 4096], P(('seq', 'fsdp'))
- up_bias_grad: float32 [4096], P(('seq', 'fsdp'))
- down_weight_grad: float32 [4096, 1024], P(('seq', 'fsdp'))
- down_bias_grad: float32 [1024], P(('seq', 'fsdp'))
The draws below stay inside these ranges and needn't reach their ends.
Inputs may be any that keep to these rules, and one draw needn't show every extreme that they name: Each row holds 4 lengths adding up to 2048; the largest is exactly 1921. `seq_order`: each row is a permutation of 0 to 3.
All inputs are finite; a program needn't handle non-finite values.
Results may differ from the reference program's by a relative error of at most 0.029.
Values may be sent and summed in bfloat16 or wider, within the bound.
No kernel may reach another device: no remote copies, remote signals or barrier semaphores. Data moves between devices by JAX's collectives and lax.ppermute only.
A program may use at most 192 MiB of HBM per device.

```python
import math
import jax
import jax.numpy as jnp
import numpy as np
from jax import lax

D = 1024
HEADS = 16
HEAD_DIM = 64
FF = 4096
SEQS = 4
GROUPS = 8
GROUP_TOK = 2048
LONGEST = 1921


def level_of(key, extent, cuts, smallest, high):
    loudness, own = 1.0, jax.random.fold_in(key, 6)
    for dim, blocks in cuts:
        heights = jnp.exp(jax.random.uniform(jax.random.fold_in(own, dim), (blocks,), jnp.float32, smallest / len(cuts), high / len(cuts)))
        loudness = loudness * jnp.repeat(heights, extent[dim] // blocks).reshape([-1 if axis == dim else 1 for axis in range(len(extent))])
    return loudness


def profile(count, total, bound, lean):
    portions = [(1 << 20) // math.isqrt(rank ** lean) + 1 for rank in range(2, count + 1)]
    surplus, given = total - bound - (count - 1), [1] * (count - 1)
    while surplus > 0:
        movable = [i for i in range(count - 1) if given[i] < bound]
        pool, left = sum([portions[i] for i in movable]), surplus
        for i in movable:
            addition = min(bound - given[i], max(1, left * portions[i] // pool), surplus)
            given[i] = given[i] + addition
            surplus = surplus - addition
    return np.array([bound] + given)


def ragged_sizes(stream_key, amount, total, limit, slope):
    if amount == 2:
        one = jax.random.randint(stream_key, (), max(1, total - limit), min(limit, total - 1) + 1)
        return jnp.stack([one, total - one])
    tallies = jnp.asarray(profile(amount, total, limit, slope), jnp.int32)
    pairs = (amount - 1) // 2
    source_of, taker = tallies[1:1 + 2 * pairs:2], tallies[2:2 + 2 * pairs:2]
    margin = jnp.minimum(source_of - 1, limit - taker)
    shifted = jax.random.randint(jax.random.fold_in(stream_key, 1), (pairs,), 0, 1 << 20) % (margin + 1)
    tallies = tallies.at[1:1 + 2 * pairs:2].set(source_of - shifted).at[2:2 + 2 * pairs:2].set(taker + shifted)
    return tallies[jax.random.permutation(jax.random.fold_in(stream_key, 2), amount)]


def normal_values(own_key, shape, width, limit, split=(), held_as=jnp.bfloat16):
    values = jax.random.normal(own_key, shape, jnp.float32) * width
    if len(split) > 0:
        values = level_of(own_key, shape, split, -0.22, 0.18) * values
    return jnp.clip(values, min=-limit, max=limit).astype(held_as)


def setup_inputs(seed: int = 0) -> dict:
    key_of = jax.random.split(jax.random.key(seed), 17)
    return {
        "inputs": normal_values(key_of[0], (GROUPS, GROUP_TOK, D), 1.0, 6.0, ((0, 8), (1, 16)), jnp.float32),
        "cotangent": normal_values(key_of[1], (GROUPS, GROUP_TOK, D), 1.0, 6.0, ((0, 8), (1, 16)), jnp.float32),
        "lengths": jax.vmap(lambda own: ragged_sizes(own, SEQS, GROUP_TOK, LONGEST, 2))(jax.random.split(key_of[2], GROUPS)).reshape((GROUPS, SEQS)).astype(jnp.int32),
        "seq_order": jax.vmap(lambda own: jax.random.permutation(own, SEQS))(jax.random.split(key_of[3], GROUPS)).reshape((GROUPS, SEQS)).astype(jnp.int32),
        "first_gain": jnp.clip(1.0 + 0.15 * jax.random.normal(key_of[4], (D,), jnp.float32), 0.25, 1.75),
        "first_shift": normal_values(key_of[5], (D,), 0.3, 4.0, ((0, 128),), jnp.float32),
        "joined_weight": normal_values(key_of[6], (D, 3 * D), D ** -0.5, 0.1875, ((0, 128),), jnp.float32),
        "joined_bias": normal_values(key_of[7], (2 * D,), 0.3, 4.0, ((0, 128),), jnp.float32),
        "dense_weight": normal_values(key_of[8], (D, D), (D // 8) ** -0.5, 0.5, ((0, 128),), jnp.float32),
        "dense_bias": normal_values(key_of[9], (D,), 0.3, 4.0, ((0, 128),), jnp.float32),
        "second_gain": jnp.clip(1.0 + 0.15 * jax.random.normal(key_of[10], (D,), jnp.float32), 0.25, 1.75),
        "second_shift": normal_values(key_of[11], (D,), 0.3, 4.0, ((0, 128),), jnp.float32),
        "up_weight": normal_values(key_of[12], (D, FF), D ** -0.5, 0.1875, ((0, 128),), jnp.float32),
        "up_bias": normal_values(key_of[13], (FF,), 0.3, 4.0, ((0, 128),), jnp.float32),
        "down_weight": normal_values(key_of[14], (FF, D), FF ** -0.5, 0.09375, ((0, 128),), jnp.float32),
        "down_bias": normal_values(key_of[15], (D,), 0.3, 4.0, ((0, 128),), jnp.float32),
    }


@jax.custom_vjp
def low(v):
    return lax.optimization_barrier(v.astype(jnp.bfloat16)).astype(jnp.float32)

@jax.custom_vjp
def low_back(v):
    return v

def low_keep(v):
    return (low(v), None)

def low_pass(kept, grad):
    return (grad,)

def back_keep(v):
    return (v, None)

def back_low(kept, grad):
    return (low(grad),)
low.defvjp(low_keep, low_pass)
low_back.defvjp(back_keep, back_low)
EPSILON = 1e-05
HIGH = lax.Precision.HIGHEST

def layer_norm(values, gain, shift):
    centred = values - lax.optimization_barrier(jnp.mean(values, axis=-1, keepdims=True))
    variance = lax.optimization_barrier(jnp.mean(centred * centred, axis=-1, keepdims=True))
    return centred * lax.rsqrt(variance + EPSILON) * gain + shift

def gelu_tanh(values):
    return 0.5 * values * (1.0 + jnp.tanh(0.7978845608028654 * (values + 0.044715 * values * values * values)))

def head_slopes():
    return jnp.exp2(-8.0 * (jnp.arange(HEADS).astype(jnp.float32) + 1.0) / HEADS)

def sequence_starts(lengths_row, order_row, position):
    picked = (order_row[:, None] == jnp.arange(SEQS, dtype=jnp.int32)[None, :]).astype(jnp.int32)
    ordered = lax.optimization_barrier(jnp.sum(picked * lengths_row[None, :], axis=1)).astype(jnp.int32)
    ends = jnp.cumsum(ordered).astype(jnp.int32)
    return lax.optimization_barrier(jnp.sum(jnp.where(position[:, None] >= ends[None, :], ordered[None, :], 0), axis=1)).astype(jnp.int32)

def attention(query_rows, key_rows, value_rows, starts):
    row_count = query_rows.shape[0]
    block_rows = math.gcd(row_count, 512)
    block_count = row_count // block_rows
    slopes = head_slopes()
    key_heads = key_rows.reshape(row_count, HEADS, HEAD_DIM)
    value_heads = value_rows.reshape(row_count, HEADS, HEAD_DIM)
    key_pos = jnp.arange(row_count, dtype=jnp.int32)

    def one_block(pieces):
        query_block, query_pos, query_start = pieces
        query_heads = query_block.reshape(block_rows, HEADS, HEAD_DIM)
        scores = jnp.einsum('qhd,khd->hqk', query_heads, key_heads, precision=HIGH) * 0.125
        distance = (query_pos[:, None] - key_pos[None, :]).astype(jnp.float32)
        scores = low_back(scores - slopes[:, None, None] * distance[None])
        allowed = (key_pos[None, :] <= query_pos[:, None]) & (key_pos[None, :] >= query_start[:, None])
        masked = jnp.where(allowed[None], scores, -1e+30)
        largest = lax.optimization_barrier(jnp.max(masked, axis=-1, keepdims=True))
        exponent = jnp.where(allowed[None], jnp.exp(masked - largest), 0.0)
        soft_weights = low(exponent / lax.optimization_barrier(jnp.sum(exponent, axis=-1, keepdims=True)))
        mixed_block = jnp.einsum('hqk,khd->qhd', soft_weights, value_heads, precision=HIGH)
        return mixed_block.reshape(block_rows, D)
    outcome = lax.map(jax.checkpoint(one_block), (query_rows.reshape(block_count, block_rows, D), key_pos.reshape(block_count, block_rows), starts.reshape(block_count, block_rows)))
    return outcome.reshape(row_count, D)

def group_forward(inputs, starts, params):
    first_gain, first_shift, joined_weight, joined_bias, dense_weight, dense_bias, second_gain, second_shift, up_weight, up_bias, down_weight, down_bias = [low(param) for param in params]
    hidden = low(layer_norm(inputs, first_gain, first_shift))
    joined_out = jnp.dot(hidden, joined_weight, precision=HIGH)
    query_rows = low(low_back(joined_out[:, 0:D] + joined_bias[0:D]))
    key_rows = low(low_back(joined_out[:, D:2 * D]))
    value_rows = low(low_back(joined_out[:, 2 * D:3 * D] + joined_bias[D:2 * D]))
    mixed_rows = low(low_back(attention(query_rows, key_rows, value_rows, starts)))
    branch = low_back(jnp.dot(mixed_rows, dense_weight, precision=HIGH) + dense_bias)
    middle = inputs + branch
    normed = low(layer_norm(middle, second_gain, second_shift))
    upward = low_back(jnp.dot(normed, up_weight, precision=HIGH) + up_bias)
    active = low(gelu_tanh(upward))
    result = low_back(jnp.dot(active, down_weight, precision=HIGH) + down_bias)
    return middle + result

def reference(inputs, cotangent, lengths, seq_order, first_gain, first_shift, joined_weight, joined_bias, dense_weight, dense_bias, second_gain, second_shift, up_weight, up_bias, down_weight, down_bias):
    params = tuple((param.astype(jnp.float32) for param in (first_gain, first_shift, joined_weight, joined_bias, dense_weight, dense_bias, second_gain, second_shift, up_weight, up_bias, down_weight, down_bias)))
    positions = jnp.arange(GROUP_TOK, dtype=jnp.int32)

    def per_group(totals, pieces):
        group_in, group_cot, group_len, group_order = pieces
        starts = sequence_starts(group_len, group_order, positions)

        def forward(values, weights):
            return group_forward(values, starts, weights)
        group_out, pullback = jax.vjp(forward, group_in.astype(jnp.float32), params)
        group_grad, weight_grads = pullback(group_cot.astype(jnp.float32))
        totals = tuple((total + extra for total, extra in zip(totals, weight_grads)))
        return (totals, (group_out, group_grad))
    zeros = tuple((jnp.zeros_like(param) for param in params))
    totals, (output, input_grad) = lax.scan(per_group, zeros, (inputs, cotangent, lengths, seq_order))
    return (output, input_grad, totals[0], totals[1], totals[2], totals[3], totals[4], totals[5], totals[6], totals[7], totals[8], totals[9], totals[10], totals[11])
```

```python
import jax
import jax.numpy as jnp
import ml_dtypes
import numpy as np
from jax import lax
from jax.experimental import pallas as pl
from jax.experimental.pallas import tpu as pltpu
from jax.sharding import Mesh, PartitionSpec as P

D = 1024
HEADS = 16
HEAD_DIM = 64
FF = 4096
SEQS = 4
TOK = 2048
OWN = 128
BLK = 256

EPSILON = 1e-05
NEG = -1e30
ALL = ("z", "y", "x", "c")
BF = jnp.bfloat16
F32 = jnp.float32
GELU_C = 0.7978845608028654


def slope_pieces():
    slopes = np.exp2(-8.0 * (np.arange(HEADS) + 1.0) / HEADS).astype(np.float32)
    pieces = []
    rest = slopes.copy()
    for _ in range(3):
        piece = rest.astype(ml_dtypes.bfloat16).astype(np.float32)
        pieces.append(piece)
        rest = rest - piece
    return np.stack(pieces, axis=1)


SLOPES = slope_pieces()


def shift_by(value, axis, step):
    size = 2 if axis == "c" else 4
    return lax.ppermute(value, axis, [(i, (i + step) % size) for i in range(size)])


def gather4(value, axis, dim):
    me = lax.axis_index(axis)
    shape = value.shape[:dim] + (4,) + value.shape[dim:]
    out = jnp.zeros(shape, value.dtype)
    parts = ((0, value),) + tuple((k, shift_by(value, axis, k)) for k in (1, -1, 2))
    for k, part in parts:
        out = lax.dynamic_update_slice_in_dim(
            out, jnp.expand_dims(part, dim), jnp.mod(me - k, 4), dim
        )
    return out


def scatter4(value, axis):
    me = lax.axis_index(axis)
    total = lax.dynamic_index_in_dim(value, me, 0, keepdims=False).astype(F32)
    for k in (1, -1, 2):
        block = lax.dynamic_index_in_dim(value, jnp.mod(me + k, 4), 0, keepdims=False)
        total = total + shift_by(block, axis, k).astype(F32)
    return total


def gather_tokens(rows):
    near = jnp.concatenate(
        [rows] + [shift_by(rows, "y", k) for k in (1, -1, 2)], axis=0
    )
    return jnp.concatenate([near, shift_by(near, "c", 1)], axis=0)


def scatter_tokens(partial):
    half = 4 * OWN
    both = partial[:half] + shift_by(partial[half:].astype(BF), "c", 1).astype(F32)
    low = both.astype(BF)
    total = both[:OWN]
    for n, k in enumerate((1, -1, 2)):
        total = total + shift_by(low[(n + 1) * OWN : (n + 2) * OWN], "y", -k).astype(F32)
    return total


def attention_forward(
    xhat, weight, gain, shift, bias_qk, bias_v, extra_q, extra_k, q_out, k_out, v_out, lse_out, mix_out, low_out, v_turned
):
    lane = lax.broadcasted_iota(jnp.int32, (BLK, 128), 1)
    for t in range(TOK // BLK):
        rows = pl.ds(t * BLK, BLK)
        hidden = (xhat[rows, :].astype(F32) * gain[...] + shift[...]).astype(BF)
        joined = jnp.dot(hidden, weight[...], preferred_element_type=F32)
        pair = joined[:, :128] + bias_qk[...]
        value = joined[:, 128:] + bias_v[...]
        q_out[rows, :] = jnp.where(lane < 64, (pair * 0.125).astype(BF), extra_q[rows, :])
        k_out[rows, :] = jnp.where(lane < 64, pltpu.roll(pair, 64, 1).astype(BF), extra_k[rows, :])
        value = jnp.where(lane < 64, value, jnp.where(lane == 64, 1.0, 0.0))
        v_out[rows, :] = value.astype(BF)
        v_turned[:, rows] = value.T.astype(BF)
    key_row = lax.broadcasted_iota(jnp.int32, (BLK, BLK), 0)
    query_col = lax.broadcasted_iota(jnp.int32, (BLK, BLK), 1)
    for b in range(TOK // BLK):
        first = b * BLK
        rows = pl.ds(first, BLK)
        queries = q_out[rows, :]
        diag = lax.dot_general(
            k_out[rows, :], queries, (((1,), (1,)), ((), ())), preferred_element_type=F32
        )
        diag = jnp.where(key_row <= query_col, diag, NEG)
        largest = jnp.max(diag, axis=0, keepdims=True)
        if b:
            before = lax.dot_general(
                k_out[0:first, :], queries, (((1,), (1,)), ((), ())), preferred_element_type=F32
            )
            largest = jnp.maximum(largest, jnp.max(before, axis=0, keepdims=True))
        acc = jnp.dot(
            v_turned[:, rows], jnp.exp(diag - largest).astype(BF), preferred_element_type=F32
        )
        if b:
            acc = acc + jnp.dot(
                v_turned[:, 0:first], jnp.exp(before - largest).astype(BF), preferred_element_type=F32
            )
        total = acc[64:65, :]
        mixed = acc[0:64, :] / total
        lse_out[:, rows] = largest + jnp.log(total)
        mix_out[:, rows] = mixed
        low_out[2 * b] = mixed[:, :128].astype(BF)
        low_out[2 * b + 1] = mixed[:, 128:].astype(BF)


def attention_backward(q_in, k_in, v_in, lse, mix, grad, out, k_turned, dk, dv):
    for t in range(TOK // BLK):
        rows = pl.ds(t * BLK, BLK)
        k_turned[:, rows] = k_in[rows, :].astype(F32).T.astype(BF)
    dk[...] = jnp.zeros_like(dk)
    dv[...] = jnp.zeros_like(dv)
    key_row = lax.broadcasted_iota(jnp.int32, (BLK, BLK), 0)
    query_col = lax.broadcasted_iota(jnp.int32, (BLK, BLK), 1)
    for b in range(TOK // BLK):
        first = b * BLK
        rows = pl.ds(first, BLK)
        queries = q_in[rows, :]
        grad_b = jnp.concatenate([grad[2 * b], grad[2 * b + 1]], axis=1)
        delta = jnp.sum(grad_b.astype(F32) * mix[:, rows], axis=0, keepdims=True)
        total = lse[:, rows]
        dq = None
        for where in (rows, pl.ds(0, first)):
            if where is not rows and not b:
                continue
            scores = lax.dot_general(
                k_in[where, :], queries, (((1,), (1,)), ((), ())), preferred_element_type=F32
            )
            soft = jnp.exp(scores - total)
            if where is rows:
                soft = jnp.where(key_row <= query_col, soft, 0.0)
            soft_grad = jnp.dot(v_in[where, 0:64], grad_b, preferred_element_type=F32)
            score_grad = (soft * (soft_grad - delta)).astype(BF)
            part = jnp.dot(k_turned[0:64, where], score_grad, preferred_element_type=F32)
            dq = part if dq is None else dq + part
            dk[where, :] += jnp.dot(score_grad, queries, preferred_element_type=F32)
            dv[where, :] += lax.dot_general(
                soft.astype(BF), grad_b, (((1,), (1,)), ((), ())), preferred_element_type=F32
            )
        dq = (dq * 0.125).astype(BF)
        out[2 * b, 0:64, :] = dq[:, :128]
        out[2 * b + 1, 0:64, :] = dq[:, 128:]
    for s in range(TOK // OWN):
        rows = pl.ds(s * OWN, OWN)
        out[s, 64:128, :] = dk[rows, :].T[0:64, :].astype(BF)
        out[s, 128:192, :] = dv[rows, :].T.astype(BF)


def whole():
    return pl.BlockSpec(memory_space=pltpu.VMEM)


def run_forward(xhat, received, gain, shift, bias_qk, bias_v, extra_q, extra_k):
    shapes = (
        ((TOK, 128), BF),
        ((TOK, 128), BF),
        ((TOK, 128), BF),
        ((1, TOK), F32),
        ((64, TOK), F32),
        ((16, 64, 128), BF),
    )
    return pl.pallas_call(
        attention_forward,
        out_shape=[jax.ShapeDtypeStruct(s, d) for s, d in shapes],
        in_specs=[whole()] * 8,
        out_specs=[whole()] * 6,
        scratch_shapes=[pltpu.VMEM((128, TOK), BF)],
        compiler_params=pltpu.CompilerParams(vmem_limit_bytes=48 * 2**20),
        name="attention_forward",
    )(xhat, received, gain, shift, bias_qk, bias_v, extra_q, extra_k)


def run_backward(q_in, k_in, v_in, lse, mix, grad):
    return pl.pallas_call(
        attention_backward,
        out_shape=jax.ShapeDtypeStruct((16, 192, 128), BF),
        in_specs=[whole()] * 6,
        out_specs=whole(),
        scratch_shapes=[
            pltpu.VMEM((128, TOK), BF),
            pltpu.VMEM((TOK, 128), F32),
            pltpu.VMEM((TOK, 64), F32),
        ],
        compiler_params=pltpu.CompilerParams(vmem_limit_bytes=48 * 2**20),
        name="attention_backward",
    )(q_in, k_in, v_in, lse, mix, grad)


def position_lanes(lengths_row, order_row, head):
    picked = (order_row[:, None] == jnp.arange(SEQS, dtype=jnp.int32)[None, :]).astype(jnp.int32)
    ordered = jnp.sum(picked * lengths_row[None, :], axis=1)
    upto = np.tril(np.ones((SEQS, SEQS), np.int32))
    ends = jnp.sum(upto * ordered[None, :], axis=1)
    position = lax.broadcasted_iota(jnp.int32, (TOK, 1), 0)
    segment = jnp.sum((position >= ends[None, :]).astype(jnp.int32), axis=1, keepdims=True)
    lane = lax.broadcasted_iota(jnp.int32, (TOK, 128), 1)
    pieces = lax.dynamic_index_in_dim(jnp.asarray(SLOPES), head, 0, keepdims=False)
    third = jnp.mod(lane - 64, 3)
    slope = jnp.where(third == 0, pieces[0], jnp.where(third == 1, pieces[1], pieces[2]))
    coarse = ((position // 256) * 256).astype(F32)
    fine = jnp.mod(position, 256).astype(F32)
    match = lane - 76 == segment
    extra_q = jnp.where(
        lane < 70,
        slope,
        jnp.where(lane < 73, -coarse, jnp.where(lane < 76, -fine, jnp.where(match, NEG, 0.0))),
    )
    extra_k = jnp.where(
        lane < 67,
        coarse,
        jnp.where(lane < 70, fine, jnp.where(lane < 76, slope, jnp.where(match, 0.0, 1.0))),
    )
    used = (lane >= 64) & (lane < 80)
    return (
        jnp.where(used, extra_q, 0.0).astype(BF),
        jnp.where(used, extra_k, 0.0).astype(BF),
    )


def normalise(values):
    centred = values - jnp.mean(values, axis=-1, keepdims=True)
    variance = jnp.mean(centred * centred, axis=-1, keepdims=True)
    scale = lax.rsqrt(variance + EPSILON)
    return centred * scale, scale


def normalise_back(grad, xhat, scale):
    return scale * (
        grad
        - jnp.mean(grad, axis=-1, keepdims=True)
        - xhat * jnp.mean(grad * xhat, axis=-1, keepdims=True)
    )


def local(
    inputs,
    cotangent,
    lengths,
    seq_order,
    first_gain,
    first_shift,
    joined_weight,
    joined_bias,
    dense_weight,
    dense_bias,
    second_gain,
    second_shift,
    up_weight,
    up_bias,
    down_weight,
    down_bias,
):
    iz, iy, ix, ic = (lax.axis_index(a) for a in ALL)
    head = iz * 4 + iy
    device = ((iz * 4 + iy) * 4 + ix) * 2 + ic

    tokens_in = inputs[0]
    xhat_one, scale_one = normalise(tokens_in)
    xhat_all = lax.all_gather(xhat_one.astype(BF), ("z", "y"), axis=0, tiled=True)

    joined_low = joined_weight.astype(BF)
    joined_heads = joined_low.reshape(8, 3, HEADS, HEAD_DIM).transpose(2, 0, 1, 3)
    joined_heads = joined_heads.reshape(4, 4, 1, 1, 8, 192)
    up_low = up_weight.astype(BF).reshape(8, 4, 4, 4, 2, 32).transpose(2, 4, 0, 3, 1, 5)
    up_low = up_low.reshape(1, 4, 1, 2, 8, 512)
    small = jnp.concatenate(
        [
            first_gain,
            first_shift,
            joined_bias,
            dense_bias,
            second_gain,
            second_shift,
            up_bias,
            down_bias,
        ]
    ).astype(BF)
    small = jnp.pad(small.reshape(8, 12), ((0, 0), (0, 52))).reshape(1, 1, 1, 1, 8, 64)
    sent = jnp.concatenate(
        [
            jnp.broadcast_to(up_low, (4, 4, 4, 2, 8, 512)),
            jnp.broadcast_to(joined_heads, (4, 4, 4, 2, 8, 192)),
            jnp.broadcast_to(small, (4, 4, 4, 2, 8, 64)),
        ],
        axis=-1,
    ).reshape(128, 8, 768)
    received = lax.all_to_all(sent, ALL, 0, 0, tiled=True).reshape(D, 768)
    up_full = received[:, :512]
    head_weight = received[:, 512:768]
    small_all = received[:, 704:716].reshape(128, 96).astype(F32)
    gain_one = small_all[:, 0:8].reshape(1, D)
    shift_one = small_all[:, 8:16].reshape(1, D)
    joined_add = small_all[:, 16:32].reshape(2, HEADS, HEAD_DIM)
    dense_add = small_all[:, 32:40].reshape(1, D)
    gain_two = small_all[:, 40:48].reshape(1, D)
    shift_two = small_all[:, 48:56].reshape(1, D)
    up_add = small_all[:, 56:88].reshape(4, 4, 4, 2, 32)
    down_add = small_all[:, 88:96].reshape(1, D)
    up_add = lax.dynamic_index_in_dim(up_add, iy, 1, keepdims=False)
    up_add = lax.dynamic_index_in_dim(up_add, ic, 2, keepdims=False)
    up_add = up_add.transpose(1, 0, 2).reshape(1, 512)

    rows_low = jnp.concatenate([down_weight.astype(BF), dense_weight.astype(BF)], axis=0)
    rows_all = gather4(gather4(rows_low, "z", 0), "x", 0)
    down_full = rows_all[:, :, :32].reshape(512, D)
    dense_near = gather4(rows_all[:, :, 32:], "y", 2)
    dense_far = shift_by(dense_near, "c", 1)
    dense_full = jnp.where(
        ic == 0, jnp.stack([dense_near, dense_far]), jnp.stack([dense_far, dense_near])
    ).reshape(D, D)

    grad_out = cotangent[0]
    res_grad = grad_out.astype(BF)
    res_all = gather_tokens(res_grad)

    extra_q, extra_k = position_lanes(lengths[0], seq_order[0], head)
    own_bias = lax.dynamic_index_in_dim(joined_add, head, 1, keepdims=False)
    nothing = jnp.zeros((64,), F32)
    bias_qk = jnp.concatenate([own_bias[0], nothing]).reshape(1, 128)
    bias_v = jnp.concatenate([own_bias[1], nothing]).reshape(1, 128)
    q_rows, k_rows, v_rows, lse, mixed, mixed_low = run_forward(
        xhat_all, head_weight, gain_one, shift_one, bias_qk, bias_v, extra_q, extra_k
    )
    mixed_own = lax.all_to_all(mixed_low, ("z", "y"), 0, 0, tiled=True)
    mixed_own = (
        mixed_own.reshape(4, 4, 4, 2, 8, OWN).transpose(3, 2, 0, 1, 4, 5).reshape(D, OWN)
    )

    branch = lax.dot_general(
        mixed_own, dense_full, (((0,), (0,)), ((), ())), preferred_element_type=F32
    )
    middle = tokens_in + branch + dense_add
    xhat_two, scale_two = normalise(middle)
    normed = (xhat_two * gain_two + shift_two).astype(BF)

    normed_all = gather_tokens(normed)
    upward = jnp.dot(normed_all, up_full, preferred_element_type=F32) + up_add
    square = upward * upward
    bend = jnp.tanh(GELU_C * upward * (1.0 + 0.044715 * square))
    active = (0.5 * upward * (1.0 + bend)).astype(BF)
    slope = 0.5 * (1.0 + bend) + 0.5 * upward * (1.0 - bend * bend) * GELU_C * (
        1.0 + 3.0 * 0.044715 * square
    )
    act_grad = lax.dot_general(
        res_all, down_full, (((1,), (1,)), ((), ())), preferred_element_type=F32
    )
    up_grad = (slope * act_grad).astype(BF)
    normed_grad = scatter_tokens(
        lax.dot_general(up_grad, up_full, (((1,), (1,)), ((), ())), preferred_element_type=F32)
    )
    result = scatter_tokens(jnp.dot(active, down_full, preferred_element_type=F32))
    output = middle + result + down_add
    up_b_grad = jnp.sum(up_grad.astype(F32), axis=0)
    up_w_grad = lax.dot_general(
        normed_all, up_grad, (((0,), (0,)), ((), ())), preferred_element_type=F32
    ).astype(BF)
    down_w_grad = lax.dot_general(
        active, res_all, (((0,), (0,)), ((), ())), preferred_element_type=F32
    ).astype(BF)

    scaled_two = gain_two * normed_grad
    middle_grad = grad_out + normalise_back(scaled_two, xhat_two, scale_two)
    branch_grad = middle_grad.astype(BF)
    mixed_grad = lax.dot_general(
        dense_full, branch_grad, (((1,), (1,)), ((), ())), preferred_element_type=F32
    ).astype(BF)
    mixed_grad = (
        mixed_grad.reshape(2, 4, 4, 4, 8, OWN).transpose(2, 3, 1, 0, 4, 5).reshape(HEADS, HEAD_DIM, OWN)
    )
    mixed_grad = lax.all_to_all(mixed_grad, ("z", "y"), 0, 0, tiled=True)
    joined_grad = run_backward(q_rows, k_rows, v_rows, lse, mixed, mixed_grad)
    joined_own = lax.all_to_all(joined_grad, ("z", "y"), 0, 0, tiled=True)

    up_blocks = up_w_grad.reshape(4, 4, 4, 2, 8, 512).transpose(2, 0, 1, 3, 4, 5)
    up_blocks = up_blocks.reshape(4, 4, 64, 512)
    down_blocks = down_w_grad.reshape(4, 4, 32, 2, 512).transpose(0, 1, 3, 2, 4)
    down_blocks = down_blocks.reshape(4, 4, 64, 512)
    bias_blocks = jnp.pad(
        up_b_grad.astype(BF).reshape(4, 4, 1, 32), ((0, 0), (0, 0), (0, 7), (0, 480))
    )
    blocks = jnp.concatenate([up_blocks, down_blocks, bias_blocks], axis=2)
    blocks = scatter4(scatter4(blocks, "x").astype(BF), "z")
    down_w_own = jnp.concatenate([blocks[64:96], blocks[96:128]], axis=1)
    up_b_own = blocks[128, :32]
    up_own = lax.all_to_all(
        blocks[:64].astype(BF).reshape(8, 8, 512), ("y", "c"), 0, 0, tiled=True
    )
    up_w_own = (
        up_own.reshape(4, 2, 8, 4, 4, 32).transpose(2, 4, 0, 3, 1, 5).reshape(8, FF).astype(F32)
    )

    dense_w_grad = jnp.dot(mixed_own, branch_grad, preferred_element_type=F32).astype(BF)
    sums = jnp.stack(
        [
            jnp.sum(res_grad.astype(F32), axis=0),
            jnp.sum(branch_grad.astype(F32), axis=0),
            jnp.sum(normed_grad * xhat_two, axis=0),
            jnp.sum(normed_grad, axis=0),
        ],
        axis=-1,
    ).astype(BF)
    sums = sums.reshape(4, 4, 4, 2, 8, 4).transpose(3, 2, 0, 1, 4, 5)
    sums = jnp.pad(sums.reshape(2, 4, 16, 8, 4), ((0, 0),) * 4 + ((0, 124),))
    dense_blocks = jnp.concatenate([dense_w_grad.reshape(2, 4, 16, 8, D), sums], axis=-1)
    mine = lax.dynamic_index_in_dim(dense_blocks, ic, 0, keepdims=False)
    theirs = lax.dynamic_index_in_dim(dense_blocks, 1 - ic, 0, keepdims=False)
    dense_blocks = (mine.astype(F32) + shift_by(theirs, "c", 1).astype(F32)).astype(BF)
    dense_blocks = scatter4(dense_blocks, "x").astype(BF)
    dense_blocks = lax.all_to_all(dense_blocks, ("z", "y"), 0, 0, tiled=True)
    dense_own = jnp.sum(dense_blocks.astype(F32), axis=0)
    sums_own = dense_own[:, D : D + 4].T

    weight_rows, _ = lax.optimization_barrier((joined_low, xhat_all))
    weight_rows = weight_rows.reshape(8, 3, HEADS, HEAD_DIM).transpose(0, 2, 1, 3).reshape(8, 3 * D)
    weight_all = lax.all_gather(weight_rows, ALL, axis=0, tiled=True)
    hidden_grad = lax.dot_general(
        joined_own.reshape(3 * D, OWN),
        weight_all,
        (((0,), (1,)), ((), ())),
        preferred_element_type=F32,
    )
    input_grad = middle_grad + normalise_back(gain_one * hidden_grad, xhat_one, scale_one)

    product = lax.dot_general(
        xhat_all.reshape(16, OWN, D),
        joined_grad,
        (((0, 1), (0, 2)), ((), ())),
        preferred_element_type=F32,
    )
    columns = jnp.sum(joined_grad.astype(F32), axis=(0, 2))
    columns = jnp.pad(columns.reshape(1, 8, 24), ((0, 0), (0, 0), (0, 40)))
    product = jnp.concatenate(
        [product.reshape(128, 8, 192), jnp.broadcast_to(columns, (128, 8, 64))], axis=-1
    ).astype(BF)
    product = lax.all_to_all(product, ALL, 0, 0, tiled=True)
    product = jnp.sum(product.reshape(HEADS, 8, 8, 256).astype(F32), axis=1)
    columns = product[:, :, 192:216].reshape(HEADS, 1, 192)
    product = product[:, :, :192]
    weight_own = joined_heads.reshape(HEADS, 8, 192).astype(F32)
    gain_own = first_gain.astype(BF).astype(F32).reshape(1, 8, 1)
    shift_own = first_shift.astype(BF).astype(F32).reshape(1, 8, 1)
    joined_w_own = gain_own * product + shift_own * columns
    joined_w_own = (
        joined_w_own.reshape(HEADS, 8, 3, HEAD_DIM).transpose(1, 2, 0, 3).reshape(8, 3 * D)
    )
    gain_one_own = jnp.sum(weight_own * product, axis=(0, 2))
    shift_one_own = jnp.sum(weight_own * columns, axis=(0, 2))
    columns = columns.reshape(HEADS, 3, HEAD_DIM)
    joined_b_own = lax.dynamic_slice_in_dim(
        jnp.concatenate([columns[:, 0].reshape(D), columns[:, 2].reshape(D)]), device * 16, 16
    )
    return (
        output[None],
        input_grad[None],
        gain_one_own,
        shift_one_own,
        joined_w_own,
        joined_b_own,
        dense_own[:, :D],
        sums_own[1],
        sums_own[2],
        sums_own[3],
        up_w_own,
        up_b_own,
        down_w_own,
        sums_own[0],
    )


def solution(mesh):
    fine = Mesh(mesh.devices.reshape(4, 4, 4, 2), ALL)
    tokens = P(("x", "c"), ("z", "y"), None)
    groups = P(("x", "c"), None)
    vector = P(ALL)
    matrix = P(ALL, None)
    return jax.shard_map(
        local,
        mesh=fine,
        in_specs=(
            tokens, tokens, groups, groups, vector, vector, matrix, vector,
            matrix, vector, vector, vector, matrix, vector, matrix, vector,
        ),
        out_specs=(
            tokens, tokens, vector, vector, matrix, vector, matrix,
            vector, vector, vector, matrix, vector, matrix, vector,
        ),
        check_vma=False,
    )
```

```python
import jax
import jax.numpy as jnp
import ml_dtypes
import numpy as np
from jax import lax
from jax.experimental import pallas as pl
from jax.experimental.pallas import tpu as pltpu
from jax.sharding import Mesh, PartitionSpec as P

D = 1024
HEADS = 16
HEAD_DIM = 64
FF = 4096
SEQS = 4
TOK = 2048
OWN = 128
HALF = 64
BLK = 256

EPSILON = 1e-05
NEG = -1e30
ALL = ("z", "y", "x", "c")
BF = jnp.bfloat16
F32 = jnp.float32
GELU_C = 0.7978845608028654
STEPS = (1, -1, 2)
NT = (((1,), (1,)), ((), ()))
TN = (((0,), (0,)), ((), ()))


def slope_pieces():
    slopes = np.exp2(-8.0 * (np.arange(HEADS) + 1.0) / HEADS).astype(np.float32)
    pieces = []
    rest = slopes.copy()
    for _ in range(3):
        piece = rest.astype(ml_dtypes.bfloat16).astype(np.float32)
        pieces.append(piece)
        rest = rest - piece
    return np.stack(pieces, axis=1)


SLOPES = slope_pieces()


def mm(a, b, dims=(((1,), (0,)), ((), ()))):
    return lax.dot_general(a, b, dims, preferred_element_type=F32)


def call(kernel, name, outs, args, scalars=0, scratch=(), flops=0, moved=0, room=52):
    in_specs = [pl.BlockSpec(memory_space=pltpu.SMEM)] * scalars
    in_specs += [pl.BlockSpec(memory_space=pltpu.VMEM)] * (len(args) - scalars)
    return pl.pallas_call(
        kernel,
        out_shape=[jax.ShapeDtypeStruct(s, d) for s, d in outs],
        in_specs=in_specs,
        out_specs=[pl.BlockSpec(memory_space=pltpu.VMEM)] * len(outs),
        scratch_shapes=[pltpu.VMEM(s, d) for s, d in scratch],
        compiler_params=pltpu.CompilerParams(vmem_limit_bytes=room * 2**20),
        cost_estimate=pl.CostEstimate(flops=flops, bytes_accessed=moved, transcendentals=0),
        name=name,
    )(*args)


def shift_by(value, axis, step):
    size = 2 if axis == "c" else 4
    return lax.ppermute(value, axis, [(i, (i + step) % size) for i in range(size)])


def after(value, *others):
    return lax.optimization_barrier((value,) + others)[0]


def ring(value, axis, late=False):
    one, two = shift_by(value, axis, 1), shift_by(value, axis, -1)
    return one, two, shift_by(after(value, one) if late else value, axis, 2)


def scatter4(value, axis, dim):
    me = lax.axis_index(axis)
    total = lax.dynamic_index_in_dim(value, me, dim, keepdims=False).astype(F32)
    for k in STEPS:
        block = lax.dynamic_index_in_dim(value, jnp.mod(me + k, 4), dim, keepdims=False)
        total = total + shift_by(block, axis, k).astype(F32)
    return total


def gather_tokens(rows, *first):
    others = ring(rows, "y")
    if first:
        rows = after(rows, *first)
    (near,) = call(
        stack_blocks, "stack_blocks", (((4 * OWN, D), BF),), (rows, *others), moved=2**21
    )
    return near, shift_by(near, "c", 1)


def scatter_tokens(own, far):
    first, *low = call(
        near_sums,
        "near_sums",
        (((OWN, D), F32),) + (((OWN, D), BF),) * 3,
        (own, shift_by(far, "c", 1)),
        moved=3 * 2**20,
    )
    return [first] + [shift_by(low[n], "y", -k) for n, k in enumerate(STEPS)], low


def first_norm(x, a_out, b_out, xhat_out, scale_out):
    centred = x[...] - jnp.mean(x[...], axis=1, keepdims=True)
    scale = lax.rsqrt(jnp.mean(centred * centred, axis=1, keepdims=True) + EPSILON)
    xhat = centred * scale
    xhat_out[...] = xhat
    scale_out[...] = scale
    a_out[...] = xhat[:HALF].astype(BF)
    b_out[...] = xhat[HALF:].astype(BF)


def head_blocks(vector, weight, up, out):
    lane = lax.broadcasted_iota(jnp.int32, (8, 32), 1)
    row = lax.broadcasted_iota(jnp.int32, (8, 32), 0)
    small = jnp.zeros((8, 32), F32)
    for n in range(vector.shape[0]):
        small = jnp.where((row == n % 8) & (lane == n // 8), vector[n], small)
    for h in range(HEADS):
        parts = [weight[:, n * D + h * 64 : n * D + h * 64 + 64] for n in range(3)]
        for n in range(8):
            d = 8 * h + n
            out[d] = jnp.concatenate(parts + [small, up[:, 32 * d : 32 * d + 32]], axis=1).astype(BF)


def stack_blocks(*refs):
    for n, out in enumerate(refs[len(refs) * 4 // 5 :]):
        for j in range(4):
            height = refs[4 * n + j].shape[0]
            out[j * height : (j + 1) * height, :] = refs[4 * n + j][...]


def attention_forward(offsets, *refs):
    pieces = refs[:8]
    weight, vectors, bias_qk, bias_v, extra_q, extra_k = refs[8:14]
    xhat, q_out, k_out, v_out, lse_out, mix_out, low_out, v_turned = refs[14:]
    for n, piece in enumerate(pieces):
        for j in range(4):
            first = pl.multiple_of(offsets[4 * n + j], HALF)
            xhat[pl.ds(first, HALF), :] = piece[j * HALF : (j + 1) * HALF, :]
    lane = lax.broadcasted_iota(jnp.int32, (BLK, 128), 1)
    for t in range(TOK // BLK):
        rows = pl.ds(t * BLK, BLK)
        hidden = (xhat[rows, :].astype(F32) * vectors[0:1, :] + vectors[1:2, :]).astype(BF)
        joined = mm(hidden, weight[...])
        pair = joined[:, :128] + bias_qk[...]
        value = joined[:, 128:] + bias_v[...]
        q_out[rows, :] = jnp.where(lane < 64, (pair * 0.125).astype(BF), extra_q[rows, :])
        k_out[rows, :] = jnp.where(lane < 64, pltpu.roll(pair, 64, 1).astype(BF), extra_k[rows, :])
        value = jnp.where(lane < 64, value, jnp.where(lane == 64, 1.0, 0.0))
        v_out[rows, :] = value.astype(BF)
        v_turned[:, rows] = value.T.astype(BF)
    key_row = lax.broadcasted_iota(jnp.int32, (BLK, BLK), 0)
    query_col = lax.broadcasted_iota(jnp.int32, (BLK, BLK), 1)
    for b in range(TOK // BLK):
        first = b * BLK
        rows = pl.ds(first, BLK)
        queries = q_out[rows, :]
        diag = jnp.where(key_row <= query_col, mm(k_out[rows, :], queries, NT), NEG)
        largest = jnp.max(diag, axis=0, keepdims=True)
        if b:
            before = mm(k_out[0:first, :], queries, NT)
            largest = jnp.maximum(largest, jnp.max(before, axis=0, keepdims=True))
        acc = mm(v_turned[:, rows], jnp.exp(diag - largest).astype(BF))
        if b:
            acc = acc + mm(v_turned[:, 0:first], jnp.exp(before - largest).astype(BF))
        total = acc[64:65, :]
        mixed = acc[0:64, :] / total
        lse_out[:, rows] = largest + jnp.log(total)
        mix_out[:, rows] = mixed
        low_out[2 * b] = mixed[:, :128].astype(BF)
        low_out[2 * b + 1] = mixed[:, 128:].astype(BF)


def attention_backward(q_in, k_in, v_in, lse, mix, grad, out, k_turned, dk, dv):
    for t in range(TOK // BLK):
        rows = pl.ds(t * BLK, BLK)
        k_turned[:, rows] = k_in[rows, :].astype(F32).T.astype(BF)
    dk[...] = jnp.zeros_like(dk)
    dv[...] = jnp.zeros_like(dv)
    key_row = lax.broadcasted_iota(jnp.int32, (BLK, BLK), 0)
    query_col = lax.broadcasted_iota(jnp.int32, (BLK, BLK), 1)
    for b in range(TOK // BLK):
        first = b * BLK
        rows = pl.ds(first, BLK)
        queries = q_in[rows, :]
        grad_b = jnp.concatenate([grad[2 * b], grad[2 * b + 1]], axis=1)
        delta = jnp.sum(grad_b.astype(F32) * mix[:, rows], axis=0, keepdims=True)
        total = lse[:, rows]
        dq = None
        for where in (rows, pl.ds(0, first)):
            if where is not rows and not b:
                continue
            soft = jnp.exp(mm(k_in[where, :], queries, NT) - total)
            if where is rows:
                soft = jnp.where(key_row <= query_col, soft, 0.0)
            soft_grad = mm(v_in[where, 0:64], grad_b)
            score_grad = (soft * (soft_grad - delta)).astype(BF)
            part = mm(k_turned[0:64, where], score_grad)
            dq = part if dq is None else dq + part
            dk[where, :] += mm(score_grad, queries)
            dv[where, :] += mm(soft.astype(BF), grad_b, NT)
        dq = (dq * 0.125).astype(BF)
        out[2 * b, 0:64, :] = dq[:, :128]
        out[2 * b + 1, 0:64, :] = dq[:, 128:]
    for s in range(TOK // OWN):
        rows = pl.ds(s * OWN, OWN)
        out[s, 64:128, :] = dk[rows, :].T[0:64, :].astype(BF)
        out[s, 128:192, :] = dv[rows, :].T.astype(BF)


def middle_norm(mixed, dense, x, vectors, middle_out, xhat_out, scale_out, normed_out):
    middle = x[...] + mm(mixed[...], dense[...], TN) + vectors[4:5, :]
    centred = middle - jnp.mean(middle, axis=1, keepdims=True)
    scale = lax.rsqrt(jnp.mean(centred * centred, axis=1, keepdims=True) + EPSILON)
    xhat = centred * scale
    middle_out[...] = middle
    xhat_out[...] = xhat
    scale_out[...] = scale
    normed_out[...] = (xhat * vectors[5:6, :] + vectors[6:7, :]).astype(BF)


def unpack_slab(slab, down, up):
    for n in range(16):
        down[32 * n : 32 * n + 32, :] = slab[64 * n : 64 * n + 32, :]
        if up is not None:
            up[32 * n : 32 * n + 32, :] = slab[64 * n + 32 : 64 * n + 64, :]


def near_sums(own, far, first_out, *low_out):
    for n in range(4):
        rows = pl.ds(n * OWN, OWN)
        total = own[rows, :].astype(F32) + far[rows, :].astype(F32)
        if n:
            low_out[n - 1][...] = total.astype(BF)
        else:
            first_out[...] = total


def feed_forward(near, far, grads_near, grads_far, slab, bias, active_out, upgrad_out, own_out, far_out, up, down):
    unpack_slab(slab, down, up)
    for t in range(4):
        rows = pl.ds(t * BLK, BLK)
        part = pl.ds(t % 2 * BLK, BLK)
        tokens, grads = ((near, grads_near), (far, grads_far))[t // 2]
        upward = mm(tokens[part, :], up[...], NT) + bias[...]
        square = upward * upward
        bend = jnp.tanh(GELU_C * upward * (1.0 + 0.044715 * square))
        active_out[rows, :] = (0.5 * upward * (1.0 + bend)).astype(BF)
        slope = 0.5 * (1.0 + bend) + (0.5 * GELU_C) * upward * (1.0 - bend * bend) * (
            1.0 + 3.0 * 0.044715 * square
        )
        up_grad = (slope * mm(grads[part, :], down[...], NT)).astype(BF)
        upgrad_out[rows, :] = up_grad
        (own_out, far_out)[t // 2][part, :] = mm(up_grad, up[...]).astype(BF)


def feed_forward_weights(places, near, far, grads_near, grads_far, active, up_grad, slab, result_out, blocks_out, bias_out, down):
    unpack_slab(slab, down, None)
    bias_out[...] = jnp.sum(up_grad[...].astype(F32), axis=0, keepdims=True)
    for z in range(4):
        lanes = slice(128 * z, 128 * z + 128)
        part = mm(active[0:512, lanes], grads_near[...], TN)
        part = (part + mm(active[512:1024, lanes], grads_far[...], TN)).astype(BF)
        up_part = mm(up_grad[0:512, lanes], near[...], TN)
        up_part = (up_part + mm(up_grad[512:1024, lanes], far[...], TN)).astype(BF)
        for x in range(4):
            blocks_out[x, z, 0:32, :] = part[32 * x : 32 * x + 32, :]
            blocks_out[x, z, 32:64, :] = up_part[32 * x : 32 * x + 32, :]
    for t in range(4):
        part = mm(active[t * BLK : (t + 1) * BLK, :], down[...]).astype(BF)
        for n in range(2):
            target = pl.ds(pl.multiple_of(places[2 * t + n], OWN), OWN)
            result_out[target, :] = part[n * OWN : (n + 1) * OWN, :]


def middle_back(own, one, two, three, xhat, scale, cotangent, vectors, dense, middle_out, branch_out, mixed_out, sums_out):
    normed_grad = own[...] + one[...].astype(F32) + two[...].astype(F32) + three[...].astype(F32)
    grad = vectors[5:6, :] * normed_grad
    back = scale[...] * (
        grad
        - jnp.mean(grad, axis=1, keepdims=True)
        - xhat[...] * jnp.mean(grad * xhat[...], axis=1, keepdims=True)
    )
    middle = cotangent[...] + back
    branch = middle.astype(BF)
    middle_out[...] = middle
    branch_out[...] = branch
    for h in range(HEADS):
        mixed_out[h] = mm(dense[h * 64 : (h + 1) * 64, :], branch, NT).astype(BF)
    sums = [
        jnp.sum(cotangent[...].astype(BF).astype(F32), axis=0, keepdims=True),
        jnp.sum(branch.astype(F32), axis=0, keepdims=True),
        jnp.sum(normed_grad * xhat[...], axis=0, keepdims=True),
        jnp.sum(normed_grad, axis=0, keepdims=True),
    ]
    row = lax.broadcasted_iota(jnp.int32, (128, D), 0)
    table = jnp.zeros((128, D), F32)
    for n, line in enumerate(sums):
        table = jnp.where(row == 68 + n, line, table)
    for n in range(8):
        sums_out[n * 128 : (n + 1) * 128, :] = table[:, n * 128 : (n + 1) * 128].T


def joined_weights(place, grad, xhat, weight, sums, up_bias, up_grad, out, turned):
    for s in range(TOK // OWN):
        turned[:, s * OWN : (s + 1) * OWN] = grad[s]
    columns = mm(jnp.ones((8, TOK), BF), turned[...], NT)[0:1, :]
    lane = lax.broadcasted_iota(jnp.int32, (BLK, 128), 1)
    element = lax.broadcasted_iota(jnp.int32, (BLK, 64), 1)
    target = 8 * (element // 16) + element % 8
    part = (element // 8) % 2
    for n in range(4):
        rows = pl.ds(n * BLK, BLK)
        product = mm(turned[...], xhat[:, n * BLK : (n + 1) * BLK])
        low = product[0:128, :].T
        high = product[128:192, :].T
        table = weight[rows, :].astype(F32)
        gain, shift = table[:, 192:193], table[:, 193:194]
        gain_grad = jnp.sum(table[:, :128] * low, axis=1, keepdims=True) + jnp.sum(
            table[:, 128:192] * high, axis=1, keepdims=True
        )
        shift_grad = jnp.sum(table[:, :128] * columns[:, :128], axis=1, keepdims=True) + jnp.sum(
            table[:, 128:192] * columns[:, 128:], axis=1, keepdims=True
        )
        position = lax.broadcasted_iota(jnp.int32, (BLK, 64), 0) + n * BLK
        line = jnp.where(n < 2, columns[:, 0:64], columns[:, 128:192])
        here = position - (n // 2) * 512 - place[0] * 32 == target
        first = jnp.sum(jnp.where(here & (part == 0), line, 0.0), axis=1, keepdims=True)
        second = jnp.sum(jnp.where(here & (part == 1), line, 0.0), axis=1, keepdims=True)
        line = up_bias[:, 128 * n : 128 * n + 128]
        position = lax.broadcasted_iota(jnp.int32, (BLK, 128), 0)
        here = (
            (position // 64 == place[1])
            & (position // 8 % 2 == place[2])
            & (position // 16 % 4 == lane // 32)
            & (position % 8 == lane % 8)
        )
        out[rows, 0:128] = (gain * low + shift * columns[:, :128]).astype(BF)
        tail = sums[rows, :]
        for k in range(4):
            part_k = jnp.where(here & (lane // 8 % 4 == k), line, 0.0)
            tail = jnp.where(lane == 72 + k, jnp.sum(part_k, axis=1, keepdims=True), tail)
        tail = jnp.where(lane == 64, gain_grad, tail)
        tail = jnp.where(lane == 65, shift_grad, tail)
        tail = jnp.where(lane == 66, first, tail)
        tail = jnp.where(lane == 67, second, tail)
        high = gain * high + shift * columns[:, 128:]
        up_part = up_grad[:, n * BLK : (n + 1) * BLK].T
        high = jnp.concatenate([high, tail[:, 64:96], up_part], axis=1)
        out[rows, 128:256] = high.astype(BF)


def joined_owner(received, weight_out, up_out, *outs):
    small = jnp.zeros((8, 128), F32)
    for h in range(HEADS):
        block = received[h * 64 : (h + 1) * 64, :].astype(F32)
        parts = [block[8 * n : 8 * n + 8, :] for n in range(8)]
        total = sum(parts[1:], parts[0])
        small = small + total[:, 128:]
        for n in range(3):
            weight_out[:, n * D + h * 64 : n * D + h * 64 + 64] = total[:, 64 * n : 64 * n + 64]
        for n in range(2):
            up_out[:, 256 * h + 128 * n : 256 * h + 128 * n + 128] = jnp.concatenate(
                [part[:, 224:256] for part in parts[4 * n : 4 * n + 4]], axis=1
            )
    small = small.T
    column = 64
    for out in outs:
        for n in range(out.shape[1] // 8):
            out[:, 8 * n : 8 * n + 8] = small[column : column + 1, :]
            column += 1


def input_back(grad, weight, xhat, scale, middle, vectors, out):
    hidden = mm(grad[...], weight[...], (((0,), (1,)), ((), ())))
    hidden = vectors[0:1, :] * hidden
    back = scale[...] * (
        hidden
        - jnp.mean(hidden, axis=1, keepdims=True)
        - xhat[...] * jnp.mean(hidden * xhat[...], axis=1, keepdims=True)
    )
    out[...] = middle[...] + back


def position_lanes(lengths_row, order_row, head):
    picked = (order_row[:, None] == jnp.arange(SEQS, dtype=jnp.int32)[None, :]).astype(jnp.int32)
    ordered = jnp.sum(picked * lengths_row[None, :], axis=1)
    upto = np.tril(np.ones((SEQS, SEQS), np.int32))
    ends = jnp.sum(upto * ordered[None, :], axis=1)
    position = lax.broadcasted_iota(jnp.int32, (TOK, 1), 0)
    segment = jnp.sum((position >= ends[None, :]).astype(jnp.int32), axis=1, keepdims=True)
    lane = lax.broadcasted_iota(jnp.int32, (TOK, 128), 1)
    pieces = lax.dynamic_index_in_dim(jnp.asarray(SLOPES), head, 0, keepdims=False)
    third = jnp.mod(lane - 64, 3)
    slope = jnp.where(third == 0, pieces[0], jnp.where(third == 1, pieces[1], pieces[2]))
    coarse = ((position // 256) * 256).astype(F32)
    fine = jnp.mod(position, 256).astype(F32)
    match = lane - 76 == segment
    extra_q = jnp.where(
        lane < 70,
        slope,
        jnp.where(lane < 73, -coarse, jnp.where(lane < 76, -fine, jnp.where(match, NEG, 0.0))),
    )
    extra_k = jnp.where(
        lane < 67,
        coarse,
        jnp.where(lane < 70, fine, jnp.where(lane < 76, slope, jnp.where(match, 0.0, 1.0))),
    )
    used = (lane >= 64) & (lane < 80)
    return (
        jnp.where(used, extra_q, 0.0).astype(BF),
        jnp.where(used, extra_k, 0.0).astype(BF),
    )


def local(
    inputs,
    cotangent,
    lengths,
    seq_order,
    first_gain,
    first_shift,
    joined_weight,
    joined_bias,
    dense_weight,
    dense_bias,
    second_gain,
    second_shift,
    up_weight,
    up_bias,
    down_weight,
    down_bias,
):
    iz, iy, ix, ic = (lax.axis_index(a) for a in ALL)
    head = iz * 4 + iy
    order = (0,) + STEPS

    tokens_in = inputs[0]
    row_a, row_b, xhat_one, scale_one = call(
        first_norm,
        "first_norm",
        (((HALF, D), BF), ((HALF, D), BF), ((OWN, D), F32), ((OWN, 1), F32)),
        (tokens_in,),
        moved=2 * 2**20,
    )
    ring_a = ring(row_a, "z")
    column_a, column_b = call(
        stack_blocks,
        "stack_blocks",
        (((BLK, D), BF), ((BLK, D), BF)),
        (row_a, *ring_a, row_b, *ring(row_b, "y", True)),
        moved=2 * 2**20,
    )
    pieces = [column_a, *ring(column_a, "y"), column_b, *ring(column_b, "z", True)]
    offsets = [
        (jnp.mod(iz - j, 4) * 4 + jnp.mod(iy - k, 4)) * OWN for k in order for j in order
    ] + [(jnp.mod(iz - k, 4) * 4 + jnp.mod(iy - j, 4)) * OWN + HALF for k in order for j in order]
    offsets = jnp.stack(offsets).astype(jnp.int32)

    joined_low = joined_weight.astype(BF)
    vector = jnp.concatenate(
        [
            first_gain,
            first_shift,
            joined_bias,
            dense_bias,
            second_gain,
            second_shift,
            up_bias,
            down_bias,
        ]
    )
    (sent,) = call(
        head_blocks,
        "head_blocks",
        (((128, 8, 256), BF),),
        (vector, joined_weight, up_weight),
        scalars=1,
        room=16,
        moved=2**20,
    )
    received = lax.all_to_all(after(sent, column_a), ALL, 0, 0, tiled=True).reshape(D, 256)
    turned = received[:, 192:256].T
    vectors = turned[:16].astype(F32)
    joined_add = vectors[2:4].reshape(2, 2, HEADS, 4, 8)
    joined_add = lax.dynamic_index_in_dim(joined_add, head, 2, keepdims=False)
    joined_add = joined_add.transpose(1, 2, 0, 3).reshape(2, 64)
    up_add = vectors[7:11].reshape(4, 4, 4, 4, 2, 8)
    up_add = lax.dynamic_index_in_dim(up_add, iy, 2, keepdims=False)
    up_add = lax.dynamic_index_in_dim(up_add, ic, 3, keepdims=False)
    up_add = up_add.transpose(1, 2, 0, 3).reshape(1, 512)

    dense_full = lax.all_gather(dense_weight.astype(BF), ALL, axis=0, tiled=True)
    extra_q, extra_k = position_lanes(lengths[0], seq_order[0], head)
    padded = jnp.pad(joined_add, ((0, 0), (0, 64)))
    vectors = after(vectors, up_add)
    xhat_all, q_rows, k_rows, v_rows, lse, mixed, mixed_low = call(
        attention_forward,
        "attention_forward",
        (
            ((TOK, D), BF),
            ((TOK, 128), BF),
            ((TOK, 128), BF),
            ((TOK, 128), BF),
            ((1, TOK), F32),
            ((64, TOK), F32),
            ((16, 64, 128), BF),
        ),
        (offsets, *pieces, received, vectors, padded[0:1], padded[1:2], extra_q, extra_k),
        scalars=1,
        scratch=(((128, TOK), BF),),
        flops=40 * 10**9,
        moved=12 * 2**20,
    )
    slab = jnp.concatenate([down_weight.astype(BF), turned[32:]], axis=0)
    slab = lax.all_gather(after(slab, mixed_low), ("z", "x"), axis=0, tiled=True)
    mixed_own = lax.all_to_all(mixed_low, ("z", "y"), 0, 0, tiled=True).reshape(D, OWN)
    middle, xhat_two, scale_two, normed = call(
        middle_norm,
        "middle_norm",
        (((OWN, D), F32), ((OWN, D), F32), ((OWN, 1), F32), ((OWN, D), BF)),
        (mixed_own, dense_full, tokens_in, vectors),
        flops=10**9,
        moved=4 * 2**20,
    )

    grad_out = cotangent[0]
    res_all = gather_tokens(after(grad_out.astype(BF), *pieces), mixed_own)
    normed_all = gather_tokens(after(normed, *res_all))
    places = [(jnp.mod(iy - k, 4) * 2 + c) * OWN for c in (ic, 1 - ic) for k in order]
    places = jnp.stack(places).astype(jnp.int32)
    active, up_grad, own, far = call(
        feed_forward,
        "feed_forward",
        (((D, 512), BF), ((D, 512), BF), ((512, D), BF), ((512, D), BF)),
        (*normed_all, *res_all, slab, up_add),
        scratch=(((512, D), BF), ((512, D), BF)),
        flops=6 * 10**9,
        moved=14 * 2**20,
    )
    terms, low = scatter_tokens(own, far)
    up_grad = after(up_grad, *low)
    result, blocks, up_b_grad = call(
        feed_forward_weights,
        "feed_forward_weights",
        (((D, D), BF), ((4, 4, 64, D), BF), ((1, 512), F32)),
        (places, *normed_all, *res_all, active, up_grad, slab),
        scalars=1,
        scratch=(((512, D), BF),),
        flops=6 * 10**9,
        moved=14 * 2**20,
    )
    middle_grad, branch_grad, mixed_grad, sums = call(
        middle_back,
        "middle_back",
        (((OWN, D), F32), ((OWN, D), BF), ((HEADS, HEAD_DIM, OWN), BF), ((D, 128), F32)),
        (after(terms[0], blocks), *terms[1:], xhat_two, scale_two, grad_out, vectors, dense_full),
        flops=10**9,
        moved=5 * 2**20,
    )
    mixed_grad = lax.all_to_all(mixed_grad, ("z", "y"), 0, 0, tiled=True)
    send = [lax.dynamic_index_in_dim(blocks, jnp.mod(ix + k, 4), 0, keepdims=False) for k in (0, *STEPS)]
    one, two = shift_by(send[1], "x", 1), shift_by(send[2], "x", -1)
    three = shift_by(send[3], "x", 2)
    (joined_grad,) = call(
        attention_backward,
        "attention_backward",
        (((16, 192, 128), BF),),
        (q_rows, k_rows, v_rows, lse, mixed, mixed_grad),
        scratch=(((128, TOK), BF), ((TOK, 128), F32), ((TOK, 64), F32)),
        flops=50 * 10**9,
        moved=4 * 2**20,
    )
    joined_own = lax.all_to_all(joined_grad, ("z", "y"), 0, 0, tiled=True)

    weight_rows = joined_low.reshape(8, 3, HEADS, HEAD_DIM).transpose(0, 2, 1, 3).reshape(8, 3 * D)
    weight_all = lax.all_gather(after(weight_rows, mixed_low), ALL, axis=0, tiled=True)
    result = after(result, branch_grad, weight_all)
    result = lax.psum_scatter(result, ("y", "c"), scatter_dimension=0, tiled=True)
    output = middle + result.astype(F32) + vectors[11:12]

    blocks = sum(b.astype(F32) for b in (send[0], one, two, three)).astype(BF)
    blocks = scatter4(blocks, "z", 0)
    down_w_own, up_own = blocks[:32], blocks[32:]

    dense_w_grad = jnp.dot(mixed_own, branch_grad, preferred_element_type=F32).astype(BF)
    dense_w_grad = dense_w_grad.reshape(4, 4, 4, 2, 8, D)
    mine = lax.dynamic_index_in_dim(dense_w_grad, ic, 3, keepdims=False)
    theirs = lax.dynamic_index_in_dim(dense_w_grad, 1 - ic, 3, keepdims=False)
    dense_blocks = (mine.astype(F32) + shift_by(theirs, "c", 1).astype(F32)).astype(BF)
    dense_blocks = scatter4(dense_blocks, "x", 2).astype(BF)

    (input_grad,) = call(
        input_back,
        "input_back",
        (((OWN, D), F32),),
        (joined_own.reshape(3 * D, OWN), weight_all, xhat_one, scale_one, middle_grad, vectors),
        flops=2 * 10**9,
        moved=9 * 2**20,
    )

    (product,) = call(
        joined_weights,
        "joined_weights",
        (((D, 256), BF),),
        (jnp.stack([head, iy, ic]).astype(jnp.int32), joined_grad, xhat_all, received, sums, up_b_grad, up_own),
        scalars=1,
        scratch=(((192, TOK), BF),),
        flops=2 * 10**9,
        moved=7 * 2**20,
    )
    product = after(product, joined_own)
    dense_blocks = scatter4(dense_blocks, "z", 0).astype(BF)
    dense_own = scatter4(dense_blocks, "y", 0)
    product = lax.all_to_all(product.reshape(128, 8, 256), ALL, 0, 0, tiled=True)
    joined_w_own, up_w_own, *vectors_grad = call(
        joined_owner,
        "joined_owner",
        (((8, 3 * D), F32), ((8, FF), F32)) + tuple(((1, n), F32) for n in (8, 8, 16, 8, 8, 8, 8, 32)),
        (after(product.reshape(D, 256), input_grad, output),),
        flops=30 * 10**9,
        moved=2**20,
    )
    gain_one_own, shift_one_own, joined_b_own, down_b_own, dense_b_own, gain_two_own, shift_two_own, up_b_own = (
        v.reshape(-1) for v in vectors_grad
    )

    return (
        output[None],
        input_grad[None],
        gain_one_own,
        shift_one_own,
        joined_w_own,
        joined_b_own,
        dense_own,
        dense_b_own,
        gain_two_own,
        shift_two_own,
        up_w_own,
        up_b_own,
        down_w_own,
        down_b_own,
    )


def solution(mesh):
    fine = Mesh(mesh.devices.reshape(4, 4, 4, 2), ALL)
    tokens = P(("x", "c"), ("z", "y"), None)
    groups = P(("x", "c"), None)
    vector = P(ALL)
    matrix = P(ALL, None)
    return jax.shard_map(
        local,
        mesh=fine,
        in_specs=(
            tokens, tokens, groups, groups, vector, vector, matrix, vector,
            matrix, vector, vector, vector, matrix, vector, matrix, vector,
        ),
        out_specs=(
            tokens, tokens, vector, vector, matrix, vector, matrix,
            vector, vector, vector, matrix, vector, matrix, vector,
        ),
        check_vma=False,
    )
```

```python
import jax
import jax.numpy as jnp
import ml_dtypes
import numpy as np
from jax import lax
from jax.experimental import pallas as pl
from jax.experimental.pallas import tpu as pltpu
from jax.sharding import Mesh, PartitionSpec as P

D = 1024
HEADS = 16
HEAD_DIM = 64
FF = 4096
SEQS = 4
TOK = 2048
OWN = 128
HALF = 64
BLK = 256

EPSILON = 1e-05
NEG = -1e30
ALL = ("z", "y", "x", "c")
BF = jnp.bfloat16
F32 = jnp.float32
GELU_C = 0.7978845608028654
STEPS = (1, -1, 2)
NT = (((1,), (1,)), ((), ()))
TN = (((0,), (0,)), ((), ()))


OPT = {'result': 2, 'wj': 0, 'dz': 0, 'ms': 0, 'm3': 1, 'mq': 0, 'dd': 0, 'mj': 0, 'dj': 1, 'mb': 0, 'fb': 25, 'ff': 40, 'fo': 30, 'ds': 0, 'dk': 2, 'hn': 0, 'l1': True, 'l2': True, 'wt': 0, 'pl': 0, 'de': 0, 'oo': 1, 'sl': 1, 'ug': 1, 'pj': 1}


def slope_pieces():
    slopes = np.exp2(-8.0 * (np.arange(HEADS) + 1.0) / HEADS).astype(np.float32)
    pieces = []
    rest = slopes.copy()
    for _ in range(3):
        piece = rest.astype(ml_dtypes.bfloat16).astype(np.float32)
        pieces.append(piece)
        rest = rest - piece
    return np.stack(pieces, axis=1)


SLOPES = slope_pieces()


def mm(a, b, dims=(((1,), (0,)), ((), ()))):
    return lax.dot_general(a, b, dims, preferred_element_type=F32)


def call(kernel, name, outs, args, scalars=0, scratch=(), flops=0, moved=0, room=52):
    in_specs = [pl.BlockSpec(memory_space=pltpu.SMEM)] * scalars
    in_specs += [pl.BlockSpec(memory_space=pltpu.VMEM)] * (len(args) - scalars)
    return pl.pallas_call(
        kernel,
        out_shape=[jax.ShapeDtypeStruct(s, d) for s, d in outs],
        in_specs=in_specs,
        out_specs=[pl.BlockSpec(memory_space=pltpu.VMEM)] * len(outs),
        scratch_shapes=[pltpu.VMEM(s, d) for s, d in scratch],
        compiler_params=pltpu.CompilerParams(vmem_limit_bytes=room * 2**20),
        cost_estimate=pl.CostEstimate(flops=flops, bytes_accessed=moved, transcendentals=0),
        name=name,
    )(*args)


def shift_by(value, axis, step):
    size = 2 if axis == "c" else 4
    return lax.ppermute(value, axis, [(i, (i + step) % size) for i in range(size)])


def after(value, *others):
    return lax.optimization_barrier((value,) + others)[0]


def ring(value, axis, late=False):
    one, two = shift_by(value, axis, 1), shift_by(value, axis, -1)
    return one, two, shift_by(after(value, one) if late else value, axis, 2)


def scatter4(value, axis, dim):
    me = lax.axis_index(axis)
    total = lax.dynamic_index_in_dim(value, me, dim, keepdims=False).astype(F32)
    for k in STEPS:
        block = lax.dynamic_index_in_dim(value, jnp.mod(me + k, 4), dim, keepdims=False)
        total = total + shift_by(block, axis, k).astype(F32)
    return total


def gather_tokens(rows, *first):
    others = ring(rows, "y")
    if first:
        rows = after(rows, *first)
    (near,) = call(
        stack_blocks, "stack_blocks", (((4 * OWN, D), BF),), (rows, *others), moved=2**21
    )
    return near, shift_by(near, "c", 1)


def scatter_tokens(own, far):
    first, *low = call(
        near_sums,
        "near_sums",
        (((OWN, D), F32),) + (((OWN, D), BF),) * 3,
        (own, shift_by(far, "c", 1)),
        moved=3 * 2**20,
    )
    return [first] + [shift_by(low[n], "y", -k) for n, k in enumerate(STEPS)], low


def first_norm(x, a_out, b_out, xhat_out, scale_out):
    centred = x[...] - jnp.mean(x[...], axis=1, keepdims=True)
    scale = lax.rsqrt(jnp.mean(centred * centred, axis=1, keepdims=True) + EPSILON)
    xhat = centred * scale
    xhat_out[...] = xhat
    scale_out[...] = scale
    a_out[...] = xhat[:HALF].astype(BF)
    b_out[...] = xhat[HALF:].astype(BF)


def head_blocks(vector, weight, up, out):
    lane = lax.broadcasted_iota(jnp.int32, (8, 32), 1)
    row = lax.broadcasted_iota(jnp.int32, (8, 32), 0)
    small = jnp.zeros((8, 32), F32)
    for n in range(vector.shape[0]):
        small = jnp.where((row == n % 8) & (lane == n // 8), vector[n], small)
    for h in range(HEADS):
        parts = [weight[:, n * D + h * 64 : n * D + h * 64 + 64] for n in range(3)]
        for n in range(8):
            d = 8 * h + n
            out[d] = jnp.concatenate(parts + [small, up[:, 32 * d : 32 * d + 32]], axis=1).astype(BF)


def stack_blocks(*refs):
    for n, out in enumerate(refs[len(refs) * 4 // 5 :]):
        for j in range(4):
            height = refs[4 * n + j].shape[0]
            out[j * height : (j + 1) * height, :] = refs[4 * n + j][...]


def attention_forward(offsets, *refs):
    pieces = refs[:8]
    weight, vectors, bias_qk, bias_v, extra_q, extra_k = refs[8:14]
    xhat, q_out, k_out, v_out, lse_out, mix_out, low_out, v_turned = refs[14:]
    for n, piece in enumerate(pieces):
        for j in range(4):
            first = pl.multiple_of(offsets[4 * n + j], HALF)
            xhat[pl.ds(first, HALF), :] = piece[j * HALF : (j + 1) * HALF, :]
    lane = lax.broadcasted_iota(jnp.int32, (BLK, 128), 1)
    for t in range(TOK // BLK):
        rows = pl.ds(t * BLK, BLK)
        hidden = (xhat[rows, :].astype(F32) * vectors[0:1, :] + vectors[1:2, :]).astype(BF)
        joined = mm(hidden, weight[...])
        pair = joined[:, :128] + bias_qk[...]
        value = joined[:, 128:] + bias_v[...]
        q_out[rows, :] = jnp.where(lane < 64, (pair * 0.125).astype(BF), extra_q[rows, :])
        k_out[rows, :] = jnp.where(lane < 64, pltpu.roll(pair, 64, 1).astype(BF), extra_k[rows, :])
        value = jnp.where(lane < 64, value, jnp.where(lane == 64, 1.0, 0.0))
        v_out[rows, :] = value.astype(BF)
        v_turned[:, rows] = value.T.astype(BF)
    key_row = lax.broadcasted_iota(jnp.int32, (BLK, BLK), 0)
    query_col = lax.broadcasted_iota(jnp.int32, (BLK, BLK), 1)
    for b in range(TOK // BLK):
        first = b * BLK
        rows = pl.ds(first, BLK)
        queries = q_out[rows, :]
        diag = jnp.where(key_row <= query_col, mm(k_out[rows, :], queries, NT), NEG)
        largest = jnp.max(diag, axis=0, keepdims=True)
        if b:
            before = mm(k_out[0:first, :], queries, NT)
            largest = jnp.maximum(largest, jnp.max(before, axis=0, keepdims=True))
        acc = mm(v_turned[:, rows], jnp.exp(diag - largest).astype(BF))
        if b:
            acc = acc + mm(v_turned[:, 0:first], jnp.exp(before - largest).astype(BF))
        total = acc[64:65, :]
        mixed = acc[0:64, :] / total
        lse_out[:, rows] = largest + jnp.log(total)
        mix_out[:, rows] = mixed
        low_out[2 * b] = mixed[:, :128].astype(BF)
        low_out[2 * b + 1] = mixed[:, 128:].astype(BF)


def attention_backward(q_in, k_in, v_in, lse, mix, grad, out, k_turned, dk, dv):
    for t in range(TOK // BLK):
        rows = pl.ds(t * BLK, BLK)
        k_turned[:, rows] = k_in[rows, :].astype(F32).T.astype(BF)
    dk[...] = jnp.zeros_like(dk)
    dv[...] = jnp.zeros_like(dv)
    key_row = lax.broadcasted_iota(jnp.int32, (BLK, BLK), 0)
    query_col = lax.broadcasted_iota(jnp.int32, (BLK, BLK), 1)
    for b in range(TOK // BLK):
        first = b * BLK
        rows = pl.ds(first, BLK)
        queries = q_in[rows, :]
        grad_b = jnp.concatenate([grad[2 * b], grad[2 * b + 1]], axis=1)
        delta = jnp.sum(grad_b.astype(F32) * mix[:, rows], axis=0, keepdims=True)
        total = lse[:, rows]
        dq = None
        for where in (rows, pl.ds(0, first)):
            if where is not rows and not b:
                continue
            soft = jnp.exp(mm(k_in[where, :], queries, NT) - total)
            if where is rows:
                soft = jnp.where(key_row <= query_col, soft, 0.0)
            soft_grad = mm(v_in[where, 0:64], grad_b)
            score_grad = (soft * (soft_grad - delta)).astype(BF)
            part = mm(k_turned[0:64, where], score_grad)
            dq = part if dq is None else dq + part
            dk[where, :] += mm(score_grad, queries)
            dv[where, :] += mm(soft.astype(BF), grad_b, NT)
        dq = (dq * 0.125).astype(BF)
        out[2 * b, 0:64, :] = dq[:, :128]
        out[2 * b + 1, 0:64, :] = dq[:, 128:]
    for s in range(TOK // OWN):
        rows = pl.ds(s * OWN, OWN)
        out[s, 64:128, :] = dk[rows, :].T[0:64, :].astype(BF)
        out[s, 128:192, :] = dv[rows, :].T.astype(BF)


def middle_norm(mixed, dense, x, vectors, middle_out, xhat_out, scale_out, normed_out):
    middle = x[...] + mm(mixed[...], dense[...], TN) + vectors[4:5, :]
    centred = middle - jnp.mean(middle, axis=1, keepdims=True)
    scale = lax.rsqrt(jnp.mean(centred * centred, axis=1, keepdims=True) + EPSILON)
    xhat = centred * scale
    middle_out[...] = middle
    xhat_out[...] = xhat
    scale_out[...] = scale
    normed_out[...] = (xhat * vectors[5:6, :] + vectors[6:7, :]).astype(BF)


def unpack_slab(slab, down, up):
    for n in range(16):
        down[32 * n : 32 * n + 32, :] = slab[64 * n : 64 * n + 32, :]
        if up is not None:
            up[32 * n : 32 * n + 32, :] = slab[64 * n + 32 : 64 * n + 64, :]


def near_sums(own, far, first_out, *low_out):
    for n in range(4):
        rows = pl.ds(n * OWN, OWN)
        total = own[rows, :].astype(F32) + far[rows, :].astype(F32)
        if n:
            low_out[n - 1][...] = total.astype(BF)
        else:
            first_out[...] = total


def feed_forward(near, far, grads_near, grads_far, slab, bias, active_out, upgrad_out, own_out, far_out, up, down):
    unpack_slab(slab, down, up)
    for t in range(4):
        rows = pl.ds(t * BLK, BLK)
        part = pl.ds(t % 2 * BLK, BLK)
        tokens, grads = ((near, grads_near), (far, grads_far))[t // 2]
        upward = mm(tokens[part, :], up[...], NT) + bias[...]
        square = upward * upward
        bend = jnp.tanh(GELU_C * upward * (1.0 + 0.044715 * square))
        active_out[rows, :] = (0.5 * upward * (1.0 + bend)).astype(BF)
        slope = 0.5 * (1.0 + bend) + (0.5 * GELU_C) * upward * (1.0 - bend * bend) * (
            1.0 + 3.0 * 0.044715 * square
        )
        up_grad = (slope * mm(grads[part, :], down[...], NT)).astype(BF)
        upgrad_out[rows, :] = up_grad
        (own_out, far_out)[t // 2][part, :] = mm(up_grad, up[...]).astype(BF)


def feed_forward_weights(places, near, far, grads_near, grads_far, active, up_grad, slab, result_out, blocks_out, bias_out, down):
    unpack_slab(slab, down, None)
    bias_out[...] = jnp.sum(up_grad[...].astype(F32), axis=0, keepdims=True)
    for z in range(4):
        lanes = slice(128 * z, 128 * z + 128)
        part = mm(active[0:512, lanes], grads_near[...], TN)
        part = (part + mm(active[512:1024, lanes], grads_far[...], TN)).astype(BF)
        up_part = mm(up_grad[0:512, lanes], near[...], TN)
        up_part = (up_part + mm(up_grad[512:1024, lanes], far[...], TN)).astype(BF)
        for x in range(4):
            blocks_out[x, z, 0:32, :] = part[32 * x : 32 * x + 32, :]
            blocks_out[x, z, 32:64, :] = up_part[32 * x : 32 * x + 32, :]
    for t in range(4):
        part = mm(active[t * BLK : (t + 1) * BLK, :], down[...]).astype(BF)
        for n in range(2):
            target = pl.ds(pl.multiple_of(places[2 * t + n], OWN), OWN)
            result_out[target, :] = part[n * OWN : (n + 1) * OWN, :]


def middle_back(own, one, two, three, xhat, scale, cotangent, vectors, dense, middle_out, branch_out, mixed_out, sums_out):
    normed_grad = own[...] + one[...].astype(F32) + two[...].astype(F32) + three[...].astype(F32)
    grad = vectors[5:6, :] * normed_grad
    back = scale[...] * (
        grad
        - jnp.mean(grad, axis=1, keepdims=True)
        - xhat[...] * jnp.mean(grad * xhat[...], axis=1, keepdims=True)
    )
    middle = cotangent[...] + back
    branch = middle.astype(BF)
    middle_out[...] = middle
    branch_out[...] = branch
    for h in range(HEADS):
        mixed_out[h] = mm(dense[h * 64 : (h + 1) * 64, :], branch, NT).astype(BF)
    sums = [
        jnp.sum(cotangent[...].astype(BF).astype(F32), axis=0, keepdims=True),
        jnp.sum(branch.astype(F32), axis=0, keepdims=True),
        jnp.sum(normed_grad * xhat[...], axis=0, keepdims=True),
        jnp.sum(normed_grad, axis=0, keepdims=True),
    ]
    row = lax.broadcasted_iota(jnp.int32, (128, D), 0)
    table = jnp.zeros((128, D), F32)
    for n, line in enumerate(sums):
        table = jnp.where(row == 68 + n, line, table)
    for n in range(8):
        sums_out[n * 128 : (n + 1) * 128, :] = table[:, n * 128 : (n + 1) * 128].T


def joined_weights(place, grad, xhat, weight, sums, up_bias, out, turned):
    for s in range(TOK // OWN):
        turned[:, s * OWN : (s + 1) * OWN] = grad[s]
    columns = mm(jnp.ones((8, TOK), BF), turned[...], NT)[0:1, :]
    lane = lax.broadcasted_iota(jnp.int32, (BLK, 128), 1)
    element = lax.broadcasted_iota(jnp.int32, (BLK, 64), 1)
    target = 8 * (element // 16) + element % 8
    part = (element // 8) % 2
    for n in range(4):
        rows = pl.ds(n * BLK, BLK)
        product = mm(turned[...], xhat[:, n * BLK : (n + 1) * BLK])
        low = product[0:128, :].T
        high = product[128:192, :].T
        table = weight[rows, :].astype(F32)
        gain, shift = table[:, 192:193], table[:, 193:194]
        gain_grad = jnp.sum(table[:, :128] * low, axis=1, keepdims=True) + jnp.sum(
            table[:, 128:192] * high, axis=1, keepdims=True
        )
        shift_grad = jnp.sum(table[:, :128] * columns[:, :128], axis=1, keepdims=True) + jnp.sum(
            table[:, 128:192] * columns[:, 128:], axis=1, keepdims=True
        )
        position = lax.broadcasted_iota(jnp.int32, (BLK, 64), 0) + n * BLK
        line = jnp.where(n < 2, columns[:, 0:64], columns[:, 128:192])
        here = position - (n // 2) * 512 - place[0] * 32 == target
        first = jnp.sum(jnp.where(here & (part == 0), line, 0.0), axis=1, keepdims=True)
        second = jnp.sum(jnp.where(here & (part == 1), line, 0.0), axis=1, keepdims=True)
        line = up_bias[:, 128 * n : 128 * n + 128]
        position = lax.broadcasted_iota(jnp.int32, (BLK, 128), 0)
        here = (
            (position // 64 == place[1])
            & (position // 8 % 2 == place[2])
            & (position // 16 % 4 == lane // 32)
            & (position % 8 == lane % 8)
        )
        out[rows, 0:128] = (gain * low + shift * columns[:, :128]).astype(BF)
        tail = sums[rows, :]
        for k in range(4):
            part_k = jnp.where(here & (lane // 8 % 4 == k), line, 0.0)
            tail = jnp.where(lane == 72 + k, jnp.sum(part_k, axis=1, keepdims=True), tail)
        tail = jnp.where(lane == 64, gain_grad, tail)
        tail = jnp.where(lane == 65, shift_grad, tail)
        tail = jnp.where(lane == 66, first, tail)
        tail = jnp.where(lane == 67, second, tail)
        high = gain * high + shift * columns[:, 128:]
        high = jnp.concatenate([high, tail[:, 64:]], axis=1)
        out[rows, 128:256] = high.astype(BF)


def join_up(product, up_grad, out):
    for n in range(4):
        rows = pl.ds(n * BLK, BLK)
        out[rows, 0:128] = product[rows, 0:128]
        up_part = up_grad[:, n * BLK : (n + 1) * BLK].T.astype(BF)
        out[rows, 128:256] = jnp.concatenate([product[rows, 128:224], up_part], axis=1)


def joined_owner(received, weight_out, up_out, *outs):
    small = jnp.zeros((8, 128), F32)
    for h in range(HEADS):
        block = received[h * 64 : (h + 1) * 64, :].astype(F32)
        parts = [block[8 * n : 8 * n + 8, :] for n in range(8)]
        total = sum(parts[1:], parts[0])
        small = small + total[:, 128:]
        for n in range(3):
            weight_out[:, n * D + h * 64 : n * D + h * 64 + 64] = total[:, 64 * n : 64 * n + 64]
        for n in range(2):
            up_out[:, 256 * h + 128 * n : 256 * h + 128 * n + 128] = jnp.concatenate(
                [part[:, 224:256] for part in parts[4 * n : 4 * n + 4]], axis=1
            )
    small = small.T
    column = 64
    for out in outs:
        for n in range(out.shape[1] // 8):
            out[:, 8 * n : 8 * n + 8] = small[column : column + 1, :]
            column += 1


def input_back(grad, weight, xhat, scale, middle, vectors, out):
    hidden = mm(grad[...], weight[...], (((0,), (1,)), ((), ())))
    hidden = vectors[0:1, :] * hidden
    back = scale[...] * (
        hidden
        - jnp.mean(hidden, axis=1, keepdims=True)
        - xhat[...] * jnp.mean(hidden * xhat[...], axis=1, keepdims=True)
    )
    out[...] = middle[...] + back


def position_lanes(lengths_row, order_row, head):
    picked = (order_row[:, None] == jnp.arange(SEQS, dtype=jnp.int32)[None, :]).astype(jnp.int32)
    ordered = jnp.sum(picked * lengths_row[None, :], axis=1)
    upto = np.tril(np.ones((SEQS, SEQS), np.int32))
    ends = jnp.sum(upto * ordered[None, :], axis=1)
    position = lax.broadcasted_iota(jnp.int32, (TOK, 1), 0)
    segment = jnp.sum((position >= ends[None, :]).astype(jnp.int32), axis=1, keepdims=True)
    lane = lax.broadcasted_iota(jnp.int32, (TOK, 128), 1)
    pieces = lax.dynamic_index_in_dim(jnp.asarray(SLOPES), head, 0, keepdims=False)
    third = jnp.mod(lane - 64, 3)
    slope = jnp.where(third == 0, pieces[0], jnp.where(third == 1, pieces[1], pieces[2]))
    coarse = ((position // 256) * 256).astype(F32)
    fine = jnp.mod(position, 256).astype(F32)
    match = lane - 76 == segment
    extra_q = jnp.where(
        lane < 70,
        slope,
        jnp.where(lane < 73, -coarse, jnp.where(lane < 76, -fine, jnp.where(match, NEG, 0.0))),
    )
    extra_k = jnp.where(
        lane < 67,
        coarse,
        jnp.where(lane < 70, fine, jnp.where(lane < 76, slope, jnp.where(match, 0.0, 1.0))),
    )
    used = (lane >= 64) & (lane < 80)
    return (
        jnp.where(used, extra_q, 0.0).astype(BF),
        jnp.where(used, extra_k, 0.0).astype(BF),
    )


def local(
    inputs,
    cotangent,
    lengths,
    seq_order,
    first_gain,
    first_shift,
    joined_weight,
    joined_bias,
    dense_weight,
    dense_bias,
    second_gain,
    second_shift,
    up_weight,
    up_bias,
    down_weight,
    down_bias,
):
    iz, iy, ix, ic = (lax.axis_index(a) for a in ALL)
    head = iz * 4 + iy
    order = (0,) + STEPS

    dense_low = dense_weight.astype(BF)
    tokens_in = inputs[0]
    row_a, row_b, xhat_one, scale_one = call(
        first_norm,
        "first_norm",
        (((HALF, D), BF), ((HALF, D), BF), ((OWN, D), F32), ((OWN, 1), F32)),
        (after(tokens_in, dense_low) if OPT["de"] else tokens_in,),
        moved=2 * 2**20,
    )
    ring_a = ring(row_a, "z")
    column_a, column_b = call(
        stack_blocks,
        "stack_blocks",
        (((BLK, D), BF), ((BLK, D), BF)),
        (row_a, *ring_a, row_b, *ring(row_b, "y", OPT["l1"])),
        moved=2 * 2**20,
    )
    pieces = [column_a, *ring(column_a, "y"), column_b, *ring(column_b, "z", OPT["l2"])]
    offsets = [
        (jnp.mod(iz - j, 4) * 4 + jnp.mod(iy - k, 4)) * OWN for k in order for j in order
    ] + [(jnp.mod(iz - k, 4) * 4 + jnp.mod(iy - j, 4)) * OWN + HALF for k in order for j in order]
    offsets = jnp.stack(offsets).astype(jnp.int32)

    joined_low = joined_weight.astype(BF)
    vector = jnp.concatenate(
        [
            first_gain,
            first_shift,
            joined_bias,
            dense_bias,
            second_gain,
            second_shift,
            up_bias,
            down_bias,
        ]
    )
    (sent,) = call(
        head_blocks,
        "head_blocks",
        (((128, 8, 256), BF),),
        (vector, joined_weight, up_weight),
        scalars=1,
        room=16,
        moved=2**20,
    )
    received = lax.all_to_all(after(sent, [column_a, ring_a[0], row_a, pieces[5]][OPT["wt"]]), ALL, 0, 0, tiled=True).reshape(D, 256)
    turned = received[:, 192:256].T
    vectors = turned[:16].astype(F32)
    joined_add = vectors[2:4].reshape(2, 2, HEADS, 4, 8)
    joined_add = lax.dynamic_index_in_dim(joined_add, head, 2, keepdims=False)
    joined_add = joined_add.transpose(1, 2, 0, 3).reshape(2, 64)
    up_add = vectors[7:11].reshape(4, 4, 4, 4, 2, 8)
    up_add = lax.dynamic_index_in_dim(up_add, iy, 2, keepdims=False)
    up_add = lax.dynamic_index_in_dim(up_add, ic, 3, keepdims=False)
    up_add = up_add.transpose(1, 2, 0, 3).reshape(1, 512)

    dense_full = lax.all_gather(dense_low, ALL, axis=0, tiled=True)
    extra_q, extra_k = position_lanes(after(lengths[0], pieces[5]) if OPT["pl"] else lengths[0], seq_order[0], head)
    padded = jnp.pad(joined_add, ((0, 0), (0, 64)))
    vectors = after(vectors, up_add)
    xhat_all, q_rows, k_rows, v_rows, lse, mixed, mixed_low = call(
        attention_forward,
        "attention_forward",
        (
            ((TOK, D), BF),
            ((TOK, 128), BF),
            ((TOK, 128), BF),
            ((TOK, 128), BF),
            ((1, TOK), F32),
            ((64, TOK), F32),
            ((16, 64, 128), BF),
        ),
        (offsets, *pieces, received, vectors, padded[0:1], padded[1:2], extra_q, extra_k),
        scalars=1,
        scratch=(((128, TOK), BF),),
        flops=OPT["ff"] * 10**9,
        moved=12 * 2**20,
    )
    slab = jnp.concatenate([down_weight.astype(BF), turned[32:]], axis=0)
    slab = lax.all_gather(after(slab, [mixed_low, pieces[5], received][OPT["sl"]]), ("z", "x"), axis=0, tiled=True)
    mixed_own = lax.all_to_all(mixed_low, ("z", "y"), 0, 0, tiled=True).reshape(D, OWN)
    middle, xhat_two, scale_two, normed = call(
        middle_norm,
        "middle_norm",
        (((OWN, D), F32), ((OWN, D), F32), ((OWN, 1), F32), ((OWN, D), BF)),
        (mixed_own, dense_full, tokens_in, vectors),
        flops=10**9,
        moved=4 * 2**20,
    )

    grad_out = cotangent[0]
    res_all = gather_tokens(
        after(grad_out.astype(BF), *[pieces, (pieces[1], pieces[2]), (mixed_low,), (mixed_own,), (column_a,)][OPT["ds"]]),
        *[(), (mixed_low,), (mixed_own,), (middle,)][OPT["dk"]],
    )
    normed_all = gather_tokens(after(normed, res_all[1]) if OPT["hn"] else normed)
    places = [(jnp.mod(iy - k, 4) * 2 + c) * OWN for c in (ic, 1 - ic) for k in order]
    places = jnp.stack(places).astype(jnp.int32)
    active, up_grad, own, far = call(
        feed_forward,
        "feed_forward",
        (((D, 512), BF), ((D, 512), BF), ((512, D), BF), ((512, D), BF)),
        (*normed_all, *res_all, slab, up_add),
        scratch=(((512, D), BF), ((512, D), BF)),
        flops=6 * 10**9,
        moved=14 * 2**20,
    )
    terms, low = scatter_tokens(own, far)
    if OPT["ug"]:
        up_grad = after(up_grad, *low)
    result, blocks, up_b_grad = call(
        feed_forward_weights,
        "feed_forward_weights",
        (((D, D), BF), ((4, 4, 64, D), BF), ((1, 512), F32)),
        (places, *normed_all, *res_all, active, up_grad, slab),
        scalars=1,
        scratch=(((512, D), BF),),
        flops=6 * 10**9,
        moved=14 * 2**20,
    )
    middle_grad, branch_grad, mixed_grad, sums = call(
        middle_back,
        "middle_back",
        (((OWN, D), F32), ((OWN, D), BF), ((HEADS, HEAD_DIM, OWN), BF), ((D, 128), F32)),
        (after(terms[0], blocks) if OPT["mb"] else terms[0], *terms[1:], xhat_two, scale_two, grad_out, vectors, dense_full),
        flops=10**9,
        moved=5 * 2**20,
    )
    mixed_grad = lax.all_to_all(mixed_grad, ("z", "y"), 0, 0, tiled=True)
    if OPT["ms"]:
        blocks = after(blocks, [branch_grad, mixed_grad][OPT["ms"] - 1])
    send = [lax.dynamic_index_in_dim(blocks, jnp.mod(ix + k, 4), 0, keepdims=False) for k in (0, *STEPS)]
    one, two = shift_by(send[1], "x", 1), shift_by(send[2], "x", -1)
    three = shift_by(after(send[3], one) if OPT["m3"] else send[3], "x", 2)
    if OPT["mq"]:
        q_rows = after(q_rows, one)
    (joined_grad,) = call(
        attention_backward,
        "attention_backward",
        (((16, 192, 128), BF),),
        (q_rows, k_rows, v_rows, lse, mixed, mixed_grad),
        scratch=(((128, TOK), BF), ((TOK, 128), F32), ((TOK, 64), F32)),
        flops=OPT["fb"] * 10**9,
        moved=4 * 2**20,
    )
    joined_own = lax.all_to_all(joined_grad, ("z", "y"), 0, 0, tiled=True)

    weight_rows = joined_low.reshape(8, 3, HEADS, HEAD_DIM).transpose(0, 2, 1, 3).reshape(8, 3 * D)
    weight_all = lax.all_gather(after(weight_rows, [mixed_low, mixed_own, middle, slab][OPT["wj"]]), ALL, axis=0, tiled=True)
    result = after(result, *[(branch_grad,), (joined_grad,), (branch_grad, weight_all), (joined_grad, weight_all), (mixed_grad,)][OPT["result"]])
    result = lax.psum_scatter(result, ("y", "c"), scatter_dimension=0, tiled=True)
    output = middle + result.astype(F32) + vectors[11:12]

    blocks = sum(b.astype(F32) for b in (after(send[0], joined_grad) if OPT["mj"] else send[0], one, two, three)).astype(BF)
    blocks = scatter4(blocks, "z", 0)
    down_w_own, up_own = blocks[:32], blocks[32:]

    dense_w_grad = jnp.dot(mixed_own, after(branch_grad, [mixed_grad, joined_grad, one][OPT["dd"] - 1]) if OPT["dd"] else branch_grad, preferred_element_type=F32).astype(BF)
    dense_w_grad = dense_w_grad.reshape(4, 4, 4, 2, 8, D)
    mine = lax.dynamic_index_in_dim(dense_w_grad, ic, 3, keepdims=False)
    theirs = lax.dynamic_index_in_dim(dense_w_grad, 1 - ic, 3, keepdims=False)
    dense_blocks = ((after(mine, joined_grad) if OPT["dj"] == 1 else after(mine, up_own) if OPT["dj"] == 2 else mine).astype(F32) + shift_by(theirs, "c", 1).astype(F32)).astype(BF)
    dense_blocks = scatter4(dense_blocks, "x", 2).astype(BF)

    (input_grad,) = call(
        input_back,
        "input_back",
        (((OWN, D), F32),),
        (joined_own.reshape(3 * D, OWN), weight_all, xhat_one, scale_one, middle_grad, vectors),
        flops=2 * 10**9,
        moved=9 * 2**20,
    )

    (product,) = call(
        joined_weights,
        "joined_weights",
        (((D, 256), BF),),
        (jnp.stack([head, iy, ic]).astype(jnp.int32), joined_grad, xhat_all, received, sums, up_b_grad),
        scalars=1,
        scratch=(((192, TOK), BF),),
        flops=2 * 10**9,
        moved=7 * 2**20,
    )
    (product,) = call(
        join_up, "join_up", (((D, 256), BF),), (after(product, joined_own) if OPT["pj"] else product, up_own), room=16, moved=2**20
    )
    dense_blocks = scatter4(after(dense_blocks, product) if OPT["dz"] else dense_blocks, "z", 0).astype(BF)
    dense_own = scatter4(dense_blocks, "y", 0)
    product = lax.all_to_all(product.reshape(128, 8, 256), ALL, 0, 0, tiled=True)
    joined_w_own, up_w_own, *vectors_grad = call(
        joined_owner,
        "joined_owner",
        (((8, 3 * D), F32), ((8, FF), F32)) + tuple(((1, n), F32) for n in (8, 8, 16, 8, 8, 8, 8, 32)),
        (after(product.reshape(D, 256), *[(), (input_grad,), (input_grad, output)][OPT["oo"]]),),
        flops=OPT["fo"] * 10**9,
        moved=2**20,
    )
    gain_one_own, shift_one_own, joined_b_own, down_b_own, dense_b_own, gain_two_own, shift_two_own, up_b_own = (
        v.reshape(-1) for v in vectors_grad
    )

    return (
        output[None],
        input_grad[None],
        gain_one_own,
        shift_one_own,
        joined_w_own,
        joined_b_own,
        dense_own,
        dense_b_own,
        gain_two_own,
        shift_two_own,
        up_w_own,
        up_b_own,
        down_w_own,
        down_b_own,
    )


def solution(mesh):
    fine = Mesh(mesh.devices.reshape(4, 4, 4, 2), ALL)
    tokens = P(("x", "c"), ("z", "y"), None)
    groups = P(("x", "c"), None)
    vector = P(ALL)
    matrix = P(ALL, None)
    return jax.shard_map(
        local,
        mesh=fine,
        in_specs=(
            tokens, tokens, groups, groups, vector, vector, matrix, vector,
            matrix, vector, vector, vector, matrix, vector, matrix, vector,
        ),
        out_specs=(
            tokens, tokens, vector, vector, matrix, vector, matrix,
            vector, vector, vector, matrix, vector, matrix, vector,
        ),
        check_vma=False,
    )
```

```python
import jax
import jax.numpy as jnp
import ml_dtypes
import numpy as np
from jax import lax
from jax.experimental import pallas as pl
from jax.experimental.pallas import tpu as pltpu
from jax.sharding import Mesh, PartitionSpec as P

D = 1024
HEADS = 16
HEAD_DIM = 64
FF = 4096
SEQS = 4
TOK = 2048
OWN = 128
HALF = 64
BLK = 256

EPSILON = 1e-05
NEG = -1e30
ALL = ("z", "y", "x", "c")
BF = jnp.bfloat16
F32 = jnp.float32
GELU_C = 0.7978845608028654
STEPS = (1, -1, 2)
NT = (((1,), (1,)), ((), ()))
TN = (((0,), (0,)), ((), ()))


OPT = {'lz': 0, 'at': 1, 'sz': 0, 'sx': 0, 'md': 0, 'ib': 0, 'fj': 2, 'result': 2, 'wj': 0, 'dz': 0, 'ms': 0, 'm3': 1, 'mq': 0, 'dd': 0, 'mj': 0, 'dj': 1, 'mb': 0, 'fb': 25, 'ff': 40, 'fo': 30, 'ds': 0, 'dk': 2, 'hn': 0, 'l1': True, 'l2': True, 'wt': 0, 'pl': 0, 'de': 0, 'oo': 1, 'sl': 1, 'ug': 1, 'pj': 1}


def slope_pieces():
    slopes = np.exp2(-8.0 * (np.arange(HEADS) + 1.0) / HEADS).astype(np.float32)
    pieces = []
    rest = slopes.copy()
    for _ in range(3):
        piece = rest.astype(ml_dtypes.bfloat16).astype(np.float32)
        pieces.append(piece)
        rest = rest - piece
    return np.stack(pieces, axis=1)


SLOPES = slope_pieces()


def mm(a, b, dims=(((1,), (0,)), ((), ()))):
    return lax.dot_general(a, b, dims, preferred_element_type=F32)


def call(kernel, name, outs, args, scalars=0, scratch=(), flops=0, moved=0, room=52, lazy=False):
    in_specs = [pl.BlockSpec(memory_space=pltpu.SMEM)] * scalars
    in_specs += [pl.BlockSpec(memory_space=pltpu.VMEM)] * (len(args) - scalars)
    return pl.pallas_call(
        kernel,
        out_shape=[jax.ShapeDtypeStruct(s, d) for s, d in outs],
        in_specs=in_specs,
        out_specs=[pl.BlockSpec() if lazy else pl.BlockSpec(memory_space=pltpu.VMEM)] * len(outs),
        scratch_shapes=[pltpu.VMEM(s, d) for s, d in scratch],
        compiler_params=pltpu.CompilerParams(vmem_limit_bytes=room * 2**20),
        cost_estimate=pl.CostEstimate(flops=flops, bytes_accessed=moved, transcendentals=0),
        name=name,
    )(*args)


def shift_by(value, axis, step):
    size = 2 if axis == "c" else 4
    return lax.ppermute(value, axis, [(i, (i + step) % size) for i in range(size)])


def after(value, *others):
    return lax.optimization_barrier((value,) + others)[0]


def ring(value, axis, late=False):
    one, two = shift_by(value, axis, 1), shift_by(value, axis, -1)
    return one, two, shift_by(after(value, one) if late else value, axis, 2)


def scatter4(value, axis, dim):
    me = lax.axis_index(axis)
    total = lax.dynamic_index_in_dim(value, me, dim, keepdims=False).astype(F32)
    for k in STEPS:
        block = lax.dynamic_index_in_dim(value, jnp.mod(me + k, 4), dim, keepdims=False)
        total = total + shift_by(block, axis, k).astype(F32)
    return total


def gather_tokens(rows, *first):
    others = ring(rows, "y")
    if first:
        rows = after(rows, *first)
    (near,) = call(
        stack_blocks, "stack_blocks", (((4 * OWN, D), BF),), (rows, *others), moved=2**21
    )
    return near, shift_by(near, "c", 1)


def scatter_tokens(own, far):
    first, *low = call(
        near_sums,
        "near_sums",
        (((OWN, D), F32),) + (((OWN, D), BF),) * 3,
        (own, shift_by(far, "c", 1)),
        moved=3 * 2**20,
    )
    return [first] + [shift_by(low[n], "y", -k) for n, k in enumerate(STEPS)], low


def first_norm(x, a_out, b_out, xhat_out, scale_out):
    centred = x[...] - jnp.mean(x[...], axis=1, keepdims=True)
    scale = lax.rsqrt(jnp.mean(centred * centred, axis=1, keepdims=True) + EPSILON)
    xhat = centred * scale
    xhat_out[...] = xhat
    scale_out[...] = scale
    a_out[...] = xhat[:HALF].astype(BF)
    b_out[...] = xhat[HALF:].astype(BF)


def head_blocks(vector, weight, up, out):
    lane = lax.broadcasted_iota(jnp.int32, (8, 32), 1)
    row = lax.broadcasted_iota(jnp.int32, (8, 32), 0)
    small = jnp.zeros((8, 32), F32)
    for n in range(vector.shape[0]):
        small = jnp.where((row == n % 8) & (lane == n // 8), vector[n], small)
    for h in range(HEADS):
        parts = [weight[:, n * D + h * 64 : n * D + h * 64 + 64] for n in range(3)]
        for n in range(8):
            d = 8 * h + n
            out[d] = jnp.concatenate(parts + [small, up[:, 32 * d : 32 * d + 32]], axis=1).astype(BF)


def stack_blocks(*refs):
    for n, out in enumerate(refs[len(refs) * 4 // 5 :]):
        for j in range(4):
            height = refs[4 * n + j].shape[0]
            out[j * height : (j + 1) * height, :] = refs[4 * n + j][...]


def attention_forward(offsets, *refs):
    pieces = refs[:8]
    weight, vectors, bias_qk, bias_v, extra_q, extra_k = refs[8:14]
    xhat, q_out, k_out, v_out, lse_out, mix_out, low_out, v_turned = refs[14:]
    for n, piece in enumerate(pieces):
        for j in range(4):
            first = pl.multiple_of(offsets[4 * n + j], HALF)
            xhat[pl.ds(first, HALF), :] = piece[j * HALF : (j + 1) * HALF, :]
    lane = lax.broadcasted_iota(jnp.int32, (BLK, 128), 1)
    for t in range(TOK // BLK):
        rows = pl.ds(t * BLK, BLK)
        hidden = (xhat[rows, :].astype(F32) * vectors[0:1, :] + vectors[1:2, :]).astype(BF)
        joined = mm(hidden, weight[...])
        pair = joined[:, :128] + bias_qk[...]
        value = joined[:, 128:] + bias_v[...]
        q_out[rows, :] = jnp.where(lane < 64, (pair * 0.125).astype(BF), extra_q[rows, :])
        k_out[rows, :] = jnp.where(lane < 64, pltpu.roll(pair, 64, 1).astype(BF), extra_k[rows, :])
        value = jnp.where(lane < 64, value, jnp.where(lane == 64, 1.0, 0.0))
        v_out[rows, :] = value.astype(BF)
        v_turned[:, rows] = value.T.astype(BF)
    key_row = lax.broadcasted_iota(jnp.int32, (BLK, BLK), 0)
    query_col = lax.broadcasted_iota(jnp.int32, (BLK, BLK), 1)
    for b in range(TOK // BLK):
        first = b * BLK
        rows = pl.ds(first, BLK)
        queries = q_out[rows, :]
        diag = jnp.where(key_row <= query_col, mm(k_out[rows, :], queries, NT), NEG)
        largest = jnp.max(diag, axis=0, keepdims=True)
        if b:
            before = mm(k_out[0:first, :], queries, NT)
            largest = jnp.maximum(largest, jnp.max(before, axis=0, keepdims=True))
        acc = mm(v_turned[:, rows], jnp.exp(diag - largest).astype(BF))
        if b:
            acc = acc + mm(v_turned[:, 0:first], jnp.exp(before - largest).astype(BF))
        total = acc[64:65, :]
        mixed = acc[0:64, :] / total
        lse_out[:, rows] = largest + jnp.log(total)
        mix_out[:, rows] = mixed
        low_out[2 * b] = mixed[:, :128].astype(BF)
        low_out[2 * b + 1] = mixed[:, 128:].astype(BF)


def attention_backward(q_in, k_in, v_in, lse, mix, grad, out, k_turned, dk, dv):
    for t in range(TOK // BLK):
        rows = pl.ds(t * BLK, BLK)
        k_turned[:, rows] = k_in[rows, :].astype(F32).T.astype(BF)
    dk[...] = jnp.zeros_like(dk)
    dv[...] = jnp.zeros_like(dv)
    key_row = lax.broadcasted_iota(jnp.int32, (BLK, BLK), 0)
    query_col = lax.broadcasted_iota(jnp.int32, (BLK, BLK), 1)
    for b in range(TOK // BLK):
        first = b * BLK
        rows = pl.ds(first, BLK)
        queries = q_in[rows, :]
        grad_b = jnp.concatenate([grad[2 * b], grad[2 * b + 1]], axis=1)
        delta = jnp.sum(grad_b.astype(F32) * mix[:, rows], axis=0, keepdims=True)
        total = lse[:, rows]
        dq = None
        for where in (rows, pl.ds(0, first)):
            if where is not rows and not b:
                continue
            soft = jnp.exp(mm(k_in[where, :], queries, NT) - total)
            if where is rows:
                soft = jnp.where(key_row <= query_col, soft, 0.0)
            soft_grad = mm(v_in[where, 0:64], grad_b)
            score_grad = (soft * (soft_grad - delta)).astype(BF)
            part = mm(k_turned[0:64, where], score_grad)
            dq = part if dq is None else dq + part
            dk[where, :] += mm(score_grad, queries)
            dv[where, :] += mm(soft.astype(BF), grad_b, NT)
        dq = (dq * 0.125).astype(BF)
        out[2 * b, 0:64, :] = dq[:, :128]
        out[2 * b + 1, 0:64, :] = dq[:, 128:]
    for s in range(TOK // OWN):
        rows = pl.ds(s * OWN, OWN)
        out[s, 64:128, :] = dk[rows, :].T[0:64, :].astype(BF)
        out[s, 128:192, :] = dv[rows, :].T.astype(BF)


def middle_norm(mixed, dense, x, vectors, middle_out, xhat_out, scale_out, normed_out):
    middle = x[...] + mm(mixed[...], dense[...], TN) + vectors[4:5, :]
    centred = middle - jnp.mean(middle, axis=1, keepdims=True)
    scale = lax.rsqrt(jnp.mean(centred * centred, axis=1, keepdims=True) + EPSILON)
    xhat = centred * scale
    middle_out[...] = middle
    xhat_out[...] = xhat
    scale_out[...] = scale
    normed_out[...] = (xhat * vectors[5:6, :] + vectors[6:7, :]).astype(BF)


def unpack_slab(slab, down, up):
    for n in range(16):
        down[32 * n : 32 * n + 32, :] = slab[64 * n : 64 * n + 32, :]
        if up is not None:
            up[32 * n : 32 * n + 32, :] = slab[64 * n + 32 : 64 * n + 64, :]


def near_sums(own, far, first_out, *low_out):
    for n in range(4):
        rows = pl.ds(n * OWN, OWN)
        total = own[rows, :].astype(F32) + far[rows, :].astype(F32)
        if n:
            low_out[n - 1][...] = total.astype(BF)
        else:
            first_out[...] = total


def feed_forward(near, far, grads_near, grads_far, slab, bias, active_out, upgrad_out, own_out, far_out, up, down):
    unpack_slab(slab, down, up)
    for t in range(4):
        rows = pl.ds(t * BLK, BLK)
        part = pl.ds(t % 2 * BLK, BLK)
        tokens, grads = ((near, grads_near), (far, grads_far))[t // 2]
        upward = mm(tokens[part, :], up[...], NT) + bias[...]
        square = upward * upward
        bend = jnp.tanh(GELU_C * upward * (1.0 + 0.044715 * square))
        active_out[rows, :] = (0.5 * upward * (1.0 + bend)).astype(BF)
        slope = 0.5 * (1.0 + bend) + (0.5 * GELU_C) * upward * (1.0 - bend * bend) * (
            1.0 + 3.0 * 0.044715 * square
        )
        up_grad = (slope * mm(grads[part, :], down[...], NT)).astype(BF)
        upgrad_out[rows, :] = up_grad
        (own_out, far_out)[t // 2][part, :] = mm(up_grad, up[...]).astype(BF)


def feed_forward_weights(places, near, far, grads_near, grads_far, active, up_grad, slab, result_out, blocks_out, bias_out, down):
    unpack_slab(slab, down, None)
    bias_out[...] = jnp.sum(up_grad[...].astype(F32), axis=0, keepdims=True)
    for z in range(4):
        lanes = slice(128 * z, 128 * z + 128)
        part = mm(active[0:512, lanes], grads_near[...], TN)
        part = (part + mm(active[512:1024, lanes], grads_far[...], TN)).astype(BF)
        up_part = mm(up_grad[0:512, lanes], near[...], TN)
        up_part = (up_part + mm(up_grad[512:1024, lanes], far[...], TN)).astype(BF)
        for x in range(4):
            blocks_out[x, z, 0:32, :] = part[32 * x : 32 * x + 32, :]
            blocks_out[x, z, 32:64, :] = up_part[32 * x : 32 * x + 32, :]
    for t in range(4):
        part = mm(active[t * BLK : (t + 1) * BLK, :], down[...]).astype(BF)
        for n in range(2):
            target = pl.ds(pl.multiple_of(places[2 * t + n], OWN), OWN)
            result_out[target, :] = part[n * OWN : (n + 1) * OWN, :]


def middle_back(own, one, two, three, xhat, scale, cotangent, vectors, dense, middle_out, branch_out, mixed_out, sums_out):
    normed_grad = own[...] + one[...].astype(F32) + two[...].astype(F32) + three[...].astype(F32)
    grad = vectors[5:6, :] * normed_grad
    back = scale[...] * (
        grad
        - jnp.mean(grad, axis=1, keepdims=True)
        - xhat[...] * jnp.mean(grad * xhat[...], axis=1, keepdims=True)
    )
    middle = cotangent[...] + back
    branch = middle.astype(BF)
    middle_out[...] = middle
    branch_out[...] = branch
    for h in range(HEADS):
        mixed_out[h] = mm(dense[h * 64 : (h + 1) * 64, :], branch, NT).astype(BF)
    sums = [
        jnp.sum(cotangent[...].astype(BF).astype(F32), axis=0, keepdims=True),
        jnp.sum(branch.astype(F32), axis=0, keepdims=True),
        jnp.sum(normed_grad * xhat[...], axis=0, keepdims=True),
        jnp.sum(normed_grad, axis=0, keepdims=True),
    ]
    row = lax.broadcasted_iota(jnp.int32, (128, D), 0)
    table = jnp.zeros((128, D), F32)
    for n, line in enumerate(sums):
        table = jnp.where(row == 68 + n, line, table)
    for n in range(8):
        sums_out[n * 128 : (n + 1) * 128, :] = table[:, n * 128 : (n + 1) * 128].T


def joined_weights(place, grad, xhat, weight, sums, up_bias, out, turned):
    for s in range(TOK // OWN):
        turned[:, s * OWN : (s + 1) * OWN] = grad[s]
    columns = mm(jnp.ones((8, TOK), BF), turned[...], NT)[0:1, :]
    lane = lax.broadcasted_iota(jnp.int32, (BLK, 128), 1)
    element = lax.broadcasted_iota(jnp.int32, (BLK, 64), 1)
    target = 8 * (element // 16) + element % 8
    part = (element // 8) % 2
    for n in range(4):
        rows = pl.ds(n * BLK, BLK)
        product = mm(turned[...], xhat[:, n * BLK : (n + 1) * BLK])
        low = product[0:128, :].T
        high = product[128:192, :].T
        table = weight[rows, :].astype(F32)
        gain, shift = table[:, 192:193], table[:, 193:194]
        gain_grad = jnp.sum(table[:, :128] * low, axis=1, keepdims=True) + jnp.sum(
            table[:, 128:192] * high, axis=1, keepdims=True
        )
        shift_grad = jnp.sum(table[:, :128] * columns[:, :128], axis=1, keepdims=True) + jnp.sum(
            table[:, 128:192] * columns[:, 128:], axis=1, keepdims=True
        )
        position = lax.broadcasted_iota(jnp.int32, (BLK, 64), 0) + n * BLK
        line = jnp.where(n < 2, columns[:, 0:64], columns[:, 128:192])
        here = position - (n // 2) * 512 - place[0] * 32 == target
        first = jnp.sum(jnp.where(here & (part == 0), line, 0.0), axis=1, keepdims=True)
        second = jnp.sum(jnp.where(here & (part == 1), line, 0.0), axis=1, keepdims=True)
        line = up_bias[:, 128 * n : 128 * n + 128]
        position = lax.broadcasted_iota(jnp.int32, (BLK, 128), 0)
        here = (
            (position // 64 == place[1])
            & (position // 8 % 2 == place[2])
            & (position // 16 % 4 == lane // 32)
            & (position % 8 == lane % 8)
        )
        out[rows, 0:128] = (gain * low + shift * columns[:, :128]).astype(BF)
        tail = sums[rows, :]
        for k in range(4):
            part_k = jnp.where(here & (lane // 8 % 4 == k), line, 0.0)
            tail = jnp.where(lane == 72 + k, jnp.sum(part_k, axis=1, keepdims=True), tail)
        tail = jnp.where(lane == 64, gain_grad, tail)
        tail = jnp.where(lane == 65, shift_grad, tail)
        tail = jnp.where(lane == 66, first, tail)
        tail = jnp.where(lane == 67, second, tail)
        high = gain * high + shift * columns[:, 128:]
        high = jnp.concatenate([high, tail[:, 64:]], axis=1)
        out[rows, 128:256] = high.astype(BF)


def join_up(product, up_grad, out):
    for n in range(4):
        rows = pl.ds(n * BLK, BLK)
        out[rows, 0:128] = product[rows, 0:128]
        up_part = up_grad[:, n * BLK : (n + 1) * BLK].T.astype(BF)
        out[rows, 128:256] = jnp.concatenate([product[rows, 128:224], up_part], axis=1)


def joined_owner(received, weight_out, up_out, *outs):
    small = jnp.zeros((8, 128), F32)
    for h in range(HEADS):
        block = received[h * 64 : (h + 1) * 64, :].astype(F32)
        parts = [block[8 * n : 8 * n + 8, :] for n in range(8)]
        total = sum(parts[1:], parts[0])
        small = small + total[:, 128:]
        for n in range(3):
            weight_out[:, n * D + h * 64 : n * D + h * 64 + 64] = total[:, 64 * n : 64 * n + 64]
        for n in range(2):
            up_out[:, 256 * h + 128 * n : 256 * h + 128 * n + 128] = jnp.concatenate(
                [part[:, 224:256] for part in parts[4 * n : 4 * n + 4]], axis=1
            )
    small = small.T
    column = 64
    for out in outs:
        for n in range(out.shape[1] // 8):
            out[:, 8 * n : 8 * n + 8] = small[column : column + 1, :]
            column += 1


def input_back(grad, weight, xhat, scale, middle, vectors, out):
    hidden = mm(grad[...], weight[...], (((0,), (1,)), ((), ())))
    hidden = vectors[0:1, :] * hidden
    back = scale[...] * (
        hidden
        - jnp.mean(hidden, axis=1, keepdims=True)
        - xhat[...] * jnp.mean(hidden * xhat[...], axis=1, keepdims=True)
    )
    out[...] = middle[...] + back


def position_lanes(lengths, order, place, slopes, q_out, k_out):
    pieces = [slopes[place[0], n] for n in range(3)]
    ends = []
    for s in range(SEQS):
        own = sum(jnp.where(order[0, s] == t, lengths[0, t], 0) for t in range(SEQS))
        ends.append(own + ends[-1] if s else own)
    lane = lax.broadcasted_iota(jnp.int32, (BLK, 128), 1)
    row = lax.broadcasted_iota(jnp.int32, (BLK, 128), 0)
    third = (lane - 64) % 3
    slope = jnp.where(third == 0, pieces[0], jnp.where(third == 1, pieces[1], pieces[2]))
    fine = row.astype(F32)
    used = (lane >= 64) & (lane < 80)
    for t in range(TOK // BLK):
        rows = pl.ds(t * BLK, BLK)
        coarse = float(t * BLK)
        position = row + t * BLK
        segment = sum((position >= end).astype(jnp.int32) for end in ends)
        match = lane - 76 == segment
        extra_q = jnp.where(lane < 76, -fine, jnp.where(match, NEG, 0.0))
        extra_q = jnp.where(lane < 70, slope, jnp.where(lane < 73, -coarse, extra_q))
        extra_k = jnp.where(lane < 76, slope, jnp.where(match, 0.0, 1.0))
        extra_k = jnp.where(lane < 67, coarse, jnp.where(lane < 70, fine, extra_k))
        q_out[rows, :] = jnp.where(used, extra_q, 0.0).astype(BF)
        k_out[rows, :] = jnp.where(used, extra_k, 0.0).astype(BF)


def local(
    inputs,
    cotangent,
    lengths,
    seq_order,
    first_gain,
    first_shift,
    joined_weight,
    joined_bias,
    dense_weight,
    dense_bias,
    second_gain,
    second_shift,
    up_weight,
    up_bias,
    down_weight,
    down_bias,
):
    iz, iy, ix, ic = (lax.axis_index(a) for a in ALL)
    head = iz * 4 + iy
    order = (0,) + STEPS

    dense_low = dense_weight.astype(BF)
    tokens_in = inputs[0]
    row_a, row_b, xhat_one, scale_one = call(
        first_norm,
        "first_norm",
        (((HALF, D), BF), ((HALF, D), BF), ((OWN, D), F32), ((OWN, 1), F32)),
        (after(tokens_in, dense_low) if OPT["de"] else tokens_in,),
        moved=2 * 2**20,
    )
    ring_a = ring(row_a, "z")
    column_a, column_b = call(
        stack_blocks,
        "stack_blocks",
        (((BLK, D), BF), ((BLK, D), BF)),
        (row_a, *ring_a, row_b, *ring(row_b, "y", OPT["l1"])),
        moved=2 * 2**20,
    )
    pieces = [column_a, *ring(column_a, "y"), column_b, *ring(column_b, "z", OPT["l2"])]
    offsets = [
        (jnp.mod(iz - j, 4) * 4 + jnp.mod(iy - k, 4)) * OWN for k in order for j in order
    ] + [(jnp.mod(iz - k, 4) * 4 + jnp.mod(iy - j, 4)) * OWN + HALF for k in order for j in order]
    offsets = jnp.stack(offsets).astype(jnp.int32)

    joined_low = joined_weight.astype(BF)
    vector = jnp.concatenate(
        [
            first_gain,
            first_shift,
            joined_bias,
            dense_bias,
            second_gain,
            second_shift,
            up_bias,
            down_bias,
        ]
    )
    (sent,) = call(
        head_blocks,
        "head_blocks",
        (((128, 8, 256), BF),),
        (vector, joined_weight, up_weight),
        scalars=1,
        room=16,
        moved=2**20,
    )
    received = lax.all_to_all(after(sent, [column_a, ring_a[0], row_a, pieces[5]][OPT["wt"]]), ALL, 0, 0, tiled=True).reshape(D, 256)
    turned = received[:, 192:256].T
    vectors = turned[:16].astype(F32)
    joined_add = vectors[2:4].reshape(2, 2, HEADS, 4, 8)
    joined_add = lax.dynamic_index_in_dim(joined_add, head, 2, keepdims=False)
    joined_add = joined_add.transpose(1, 2, 0, 3).reshape(2, 64)
    up_add = vectors[7:11].reshape(4, 4, 4, 4, 2, 8)
    up_add = lax.dynamic_index_in_dim(up_add, iy, 2, keepdims=False)
    up_add = lax.dynamic_index_in_dim(up_add, ic, 3, keepdims=False)
    up_add = up_add.transpose(1, 2, 0, 3).reshape(1, 512)

    dense_full = lax.all_gather(dense_low, ALL, axis=0, tiled=True)
    extra_q, extra_k = call(
        position_lanes,
        "position_lanes",
        (((TOK, 128), BF), ((TOK, 128), BF)),
        (after(lengths, pieces[5]) if OPT["pl"] else lengths, seq_order, head.reshape(1), jnp.asarray(SLOPES)),
        scalars=4,
        room=16,
    )
    padded = jnp.pad(joined_add, ((0, 0), (0, 64)))
    vectors = after(vectors, up_add)
    xhat_all, q_rows, k_rows, v_rows, lse, mixed, mixed_low = call(
        attention_forward,
        "attention_forward",
        (
            ((TOK, D), BF),
            ((TOK, 128), BF),
            ((TOK, 128), BF),
            ((TOK, 128), BF),
            ((1, TOK), F32),
            ((64, TOK), F32),
            ((16, 64, 128), BF),
        ),
        (offsets, *pieces, received, vectors, padded[0:1], padded[1:2], extra_q, extra_k),
        scalars=1,
        scratch=(((128, TOK), BF),),
        lazy=bool(OPT["lz"]),
        flops=OPT["ff"] * 10**9,
        moved=12 * 2**20,
    )
    slab = jnp.concatenate([down_weight.astype(BF), turned[32:]], axis=0)
    slab = lax.all_gather(after(slab, [mixed_low, pieces[5], received][OPT["sl"]]), ("z", "x"), axis=0, tiled=True)
    mixed_own = lax.all_to_all(mixed_low, ("z", "y"), 0, 0, tiled=True).reshape(D, OWN)
    middle, xhat_two, scale_two, normed = call(
        middle_norm,
        "middle_norm",
        (((OWN, D), F32), ((OWN, D), F32), ((OWN, 1), F32), ((OWN, D), BF)),
        (mixed_own, dense_full, tokens_in, vectors),
        lazy=bool(OPT["lz"]),
        flops=10**9,
        moved=4 * 2**20,
    )

    grad_out = cotangent[0]
    res_all = gather_tokens(
        after(grad_out.astype(BF), *[pieces, (pieces[1], pieces[2]), (mixed_low,), (mixed_own,), (column_a,)][OPT["ds"]]),
        *[(), (mixed_low,), (mixed_own,), (middle,)][OPT["dk"]],
    )
    normed_all = gather_tokens(after(normed, res_all[1]) if OPT["hn"] else normed)
    places = [(jnp.mod(iy - k, 4) * 2 + c) * OWN for c in (ic, 1 - ic) for k in order]
    places = jnp.stack(places).astype(jnp.int32)
    active, up_grad, own, far = call(
        feed_forward,
        "feed_forward",
        (((D, 512), BF), ((D, 512), BF), ((512, D), BF), ((512, D), BF)),
        (*normed_all, *res_all, slab, up_add),
        scratch=(((512, D), BF), ((512, D), BF)),
        lazy=bool(OPT["lz"]),
        flops=6 * 10**9,
        moved=14 * 2**20,
    )
    terms, low = scatter_tokens(own, far)
    if OPT["ug"]:
        up_grad = after(up_grad, *low)
    result, blocks, up_b_grad = call(
        feed_forward_weights,
        "feed_forward_weights",
        (((D, D), BF), ((4, 4, 64, D), BF), ((1, 512), F32)),
        (places, *normed_all, *res_all, active, up_grad, slab),
        scalars=1,
        scratch=(((512, D), BF),),
        lazy=bool(OPT["lz"]),
        flops=6 * 10**9,
        moved=14 * 2**20,
    )
    middle_grad, branch_grad, mixed_grad, sums = call(
        middle_back,
        "middle_back",
        (((OWN, D), F32), ((OWN, D), BF), ((HEADS, HEAD_DIM, OWN), BF), ((D, 128), F32)),
        (after(terms[0], blocks) if OPT["mb"] else terms[0], *terms[1:], xhat_two, scale_two, grad_out, vectors, dense_full),
        flops=10**9,
        moved=5 * 2**20,
    )
    mixed_grad = lax.all_to_all(mixed_grad, ("z", "y"), 0, 0, tiled=True)
    if OPT["ms"]:
        blocks = after(blocks, [branch_grad, mixed_grad][OPT["ms"] - 1])
    send = [lax.dynamic_index_in_dim(blocks, jnp.mod(ix + k, 4), 0, keepdims=False) for k in (0, *STEPS)]
    one, two = shift_by(send[1], "x", 1), shift_by(send[2], "x", -1)
    three = shift_by(after(send[3], one) if OPT["m3"] else send[3], "x", 2)
    if OPT["mq"]:
        q_rows = after(q_rows, one)
    (joined_grad,) = call(
        attention_backward,
        "attention_backward",
        (((16, 192, 128), BF),),
        (q_rows, k_rows, v_rows, lse, mixed, mixed_grad),
        scratch=(((128, TOK), BF), ((TOK, 128), F32), ((TOK, 64), F32)),
        flops=OPT["fb"] * 10**9,
        moved=4 * 2**20,
    )
    joined_own = lax.all_to_all(joined_grad, ("z", "y"), 0, 0, tiled=True)

    weight_rows = joined_low.reshape(8, 3, HEADS, HEAD_DIM).transpose(0, 2, 1, 3).reshape(8, 3 * D)
    weight_all = lax.all_gather(after(weight_rows, [mixed_low, mixed_own, middle, slab][OPT["wj"]]), ALL, axis=0, tiled=True)
    result = after(result, *[(branch_grad,), (joined_grad,), (branch_grad, weight_all), (joined_grad, weight_all), (mixed_grad,)][OPT["result"]])
    result = lax.psum_scatter(result, ("y", "c"), scatter_dimension=0, tiled=True)
    output = middle + result.astype(F32) + vectors[11:12]

    (product,) = call(
        joined_weights,
        "joined_weights",
        (((D, 256), BF),),
        (jnp.stack([head, iy, ic]).astype(jnp.int32), joined_grad, xhat_all, received, sums, up_b_grad),
        scalars=1,
        scratch=(((192, TOK), BF),),
        flops=OPT["fj"] * 10**9,
        moved=7 * 2**20,
    )

    blocks = sum(b.astype(F32) for b in (after(send[0], *[(), (joined_grad,), (product,)][OPT["mj"]]), one, two, three)).astype(BF)
    blocks = scatter4(blocks, "z", 0)
    down_w_own, up_own = blocks[:32], blocks[32:]

    dense_w_grad = jnp.dot(mixed_own, after(branch_grad, [mixed_grad, joined_grad, one][OPT["dd"] - 1]) if OPT["dd"] else branch_grad, preferred_element_type=F32).astype(BF)
    dense_w_grad = dense_w_grad.reshape(4, 4, 4, 2, 8, D)
    mine = lax.dynamic_index_in_dim(dense_w_grad, ic, 3, keepdims=False)
    theirs = lax.dynamic_index_in_dim(dense_w_grad, 1 - ic, 3, keepdims=False)
    dense_blocks = (after(mine, *[(), (joined_grad,), (up_own,), (product,)][OPT["dj"]]).astype(F32) + shift_by(theirs, "c", 1).astype(F32)).astype(BF)
    dense_blocks = scatter4(dense_blocks, "x", 2).astype(BF)

    (input_grad,) = call(
        input_back,
        "input_back",
        (((OWN, D), F32),),
        (after(joined_own.reshape(3 * D, OWN), *[(), (product,), (up_own,), (dense_blocks,)][OPT["ib"]]), weight_all, xhat_one, scale_one, middle_grad, vectors),
        flops=2 * 10**9,
        moved=9 * 2**20,
    )

    (product,) = call(
        join_up, "join_up", (((D, 256), BF),), (after(product, joined_own) if OPT["pj"] else product, up_own), room=16, moved=2**20
    )
    dense_blocks = scatter4(after(dense_blocks, *[(), (product,), (joined_own,), (up_own,)][OPT["dz"]]), "z", 0).astype(BF)
    dense_own = scatter4(dense_blocks, "y", 0)
    product = lax.all_to_all(product.reshape(128, 8, 256), ALL, 0, 0, tiled=True)
    joined_w_own, up_w_own, *vectors_grad = call(
        joined_owner,
        "joined_owner",
        (((8, 3 * D), F32), ((8, FF), F32)) + tuple(((1, n), F32) for n in (8, 8, 16, 8, 8, 8, 8, 32)),
        (after(product.reshape(D, 256), *[(), (input_grad,), (input_grad, output)][OPT["oo"]]),),
        flops=OPT["fo"] * 10**9,
        moved=2**20,
    )
    gain_one_own, shift_one_own, joined_b_own, down_b_own, dense_b_own, gain_two_own, shift_two_own, up_b_own = (
        v.reshape(-1) for v in vectors_grad
    )

    return (
        output[None],
        input_grad[None],
        gain_one_own,
        shift_one_own,
        joined_w_own,
        joined_b_own,
        dense_own,
        dense_b_own,
        gain_two_own,
        shift_two_own,
        up_w_own,
        up_b_own,
        down_w_own,
        down_b_own,
    )


def solution(mesh):
    fine = Mesh(mesh.devices.reshape(4, 4, 4, 2), ALL)
    tokens = P(("x", "c"), ("z", "y"), None)
    groups = P(("x", "c"), None)
    vector = P(ALL)
    matrix = P(ALL, None)
    return jax.shard_map(
        local,
        mesh=fine,
        in_specs=(
            tokens, tokens, groups, groups, vector, vector, matrix, vector,
            matrix, vector, vector, vector, matrix, vector, matrix, vector,
        ),
        out_specs=(
            tokens, tokens, vector, vector, matrix, vector, matrix,
            vector, vector, vector, matrix, vector, matrix, vector,
        ),
        check_vma=False,
    )
```
